32 devices in a mesh: seq: 8 (over z, core), tp: 4 (over y, x).
Axes of the slice: x: 2, y: 2, z: 4, core: 2. Of those that a mesh axis runs over, the one named last changes fastest.
Arguments:
- queries: bfloat16 [4096, 6144], P(('seq', 'tp')), may hold values from -6 to 6
- keys: bfloat16 [4096, 6144], P(('seq', 'tp')), may hold values from -1.25 to 1.25
- values: bfloat16 [4096, 6144], P(('seq', 'tp')), may hold values from -6 to 6
- decay_rates: float32 [48], P('tp'), may hold values from 1e-05 to 0.03
- norm_gain: float32 [6144], P('tp'), may hold values from 0.25 to 1.75
- out_weight: bfloat16 [6144, 6144], P('tp'), may hold values from -0.078125 to 0.078125
- doc_lengths: int32 [32], replicated, may hold values from 1 to 2048, 4096 in all
Outputs:
- mixed: bfloat16 [4096, 6144], P(('seq', 'tp'))
The draws below stay inside these ranges and needn't reach their ends.
All inputs are finite; a program needn't handle non-finite values.
Results may differ from the reference program's by a relative error of at most 0.014.
Values may be sent and summed in bfloat16 or wider, within the bound.
A program may use at most 128 MiB of HBM per device.

```python
import math
import jax
import jax.numpy as jnp
import numpy as np
from jax import lax

D = 6144
HEADS = 48
HEAD_DIM = 128
NDOC = 32
TOKENS = 4096
N_TP = 4


def draw_decay_rates(key, part):
    key = jax.random.fold_in(key, 11)
    first_key = jax.random.fold_in(key, 0)
    return jnp.exp(jax.random.uniform(first_key, (HEADS,), jnp.float32, math.log(1e-05), math.log(0.03))).astype(jnp.float32)


def block_levels(key, extent, cuts, smallest, high):
    level, own = 1.0, jax.random.fold_in(key, 6)
    for dim, parts in cuts:
        steps = jnp.exp(jax.random.uniform(jax.random.fold_in(own, dim), (parts,), jnp.float32, smallest / len(cuts), high / len(cuts)))
        level = level * jnp.repeat(steps, extent[dim] // parts).reshape([-1 if axis == dim else 1 for axis in range(len(extent))])
    return level


def length_profile(number_of, total, most, slope):
    loads = [(1 << 20) // math.isqrt(grade ** slope) + 1 for grade in range(2, number_of + 1)]
    surplus, counts = total - most - (number_of - 1), [1] * (number_of - 1)
    while surplus > 0:
        candidates = [i for i in range(number_of - 1) if counts[i] < most]
        whole, remaining = sum([loads[i] for i in candidates]), surplus
        for i in candidates:
            addition = min(most - counts[i], max(1, remaining * loads[i] // whole), surplus)
            counts[i] = counts[i] + addition
            surplus = surplus - addition
    return np.array([most] + counts)


def uneven(rng, count, total, most, skew):
    if count == 2:
        one = jax.random.randint(rng, (), max(1, total - most), min(most, total - 1) + 1)
        return jnp.stack([one, total - one])
    tallies = jnp.asarray(length_profile(count, total, most, skew), jnp.int32)
    twos = (count - 1) // 2
    donor, taker = tallies[1:1 + 2 * twos:2], tallies[2:2 + 2 * twos:2]
    slack = jnp.minimum(donor - 1, most - taker)
    moved = jax.random.randint(jax.random.fold_in(rng, 1), (twos,), 0, 1 << 20) % (slack + 1)
    tallies = tallies.at[1:1 + 2 * twos:2].set(donor - moved).at[2:2 + 2 * twos:2].set(taker + moved)
    return tallies[jax.random.permutation(jax.random.fold_in(rng, 2), count)]


def noise(key, dims, deviation, limit, cuts=(), kind=jnp.bfloat16):
    drawn = jax.random.normal(key, dims, jnp.float32) * deviation
    if len(cuts) > 0:
        drawn = block_levels(key, dims, cuts, -0.22, 0.18) * drawn
    return jnp.clip(drawn, min=-limit, max=limit).astype(kind)


def setup_inputs(seed: int = 0) -> dict:
    key_of = jax.random.split(jax.random.key(seed), 8)
    return {
        "queries": noise(key_of[0], (TOKENS, HEADS * HEAD_DIM), 1.0, 6.0, ((0, 32),)),
        "keys": noise(key_of[1], (TOKENS, HEADS * HEAD_DIM), 0.09, 1.25, ((0, 32),)),
        "values": noise(key_of[2], (TOKENS, HEADS * HEAD_DIM), 1.0, 6.0, ((0, 32),)),
        "decay_rates": draw_decay_rates(jax.random.fold_in(key_of[7], 71), 0),
        "norm_gain": jnp.clip(1.0 + 0.15 * jax.random.normal(key_of[4], (HEADS * HEAD_DIM,), jnp.float32), 0.25, 1.75),
        "out_weight": noise(key_of[5], (HEADS * HEAD_DIM, D), (HEADS * HEAD_DIM) ** -0.5, 0.078125, ((0, 4),)),
        "doc_lengths": uneven(key_of[6], NDOC, TOKENS, TOKENS // 2, 2).astype(jnp.int32),
    }


def local_pass(q_heads, k_heads, v_heads, segments, decay_rates, seg_start):
    highest = lax.Precision.HIGHEST
    total_rows, heads_dev, head_dim = q_heads.shape
    block_rows = min(256, total_rows)
    block_count = total_rows // block_rows

    def regroup(tensor):
        return tensor.reshape(block_count, block_rows, heads_dev, head_dim)
    offsets = jnp.arange(block_rows).astype(jnp.float32)
    distance = offsets[:, None] - offsets[None, :]
    causal = distance >= 0

    def advance(running, pieces):
        kv_state, prev_seg, decay_total = running
        q_blk, k_blk, v_blk, seg_blk = pieces
        allowed = causal & (seg_blk[:, None] == seg_blk[None, :])
        decay_mat = jnp.where(allowed[None], jnp.exp(-decay_rates[:, None, None] * jnp.maximum(distance, 0.0)[None]), 0.0)
        scores = jnp.einsum('thd,shd->hts', q_blk, k_blk, precision=highest)
        weighted = lax.optimization_barrier((scores * decay_mat).astype(jnp.bfloat16)).astype(jnp.float32)
        inside = jnp.einsum('hts,shd->thd', weighted, v_blk, precision=highest)
        carry_in = jnp.where((seg_blk == prev_seg)[None, :], jnp.exp(-decay_rates[:, None] * (offsets + 1.0)[None, :]), 0.0)
        carried = jnp.einsum('thd,hde->the', q_blk, kv_state, precision=highest)
        attended = inside + carried * carry_in.T[:, :, None]
        last_seg = seg_blk[-1]
        keep_end = jnp.where((seg_blk == last_seg)[None, :], jnp.exp(-decay_rates[:, None] * (block_rows - 1.0 - offsets)[None, :]), 0.0)
        whole_keep = jnp.where(last_seg == prev_seg, jnp.exp(-decay_rates * block_rows), 0.0)
        weighted_keys = lax.optimization_barrier((k_blk * keep_end.T[:, :, None]).astype(jnp.bfloat16)).astype(jnp.float32)
        kv_state = whole_keep[:, None, None] * kv_state + jnp.einsum('shd,she->hde', weighted_keys, v_blk, precision=highest)
        return ((kv_state, last_seg, decay_total * whole_keep), attended)
    initial = (jnp.zeros((heads_dev, head_dim, head_dim), jnp.float32), seg_start, jnp.ones((heads_dev,), jnp.float32))
    finished, attended = lax.scan(advance, initial, (regroup(q_heads), regroup(k_heads), regroup(v_heads), segments.reshape(block_count, block_rows)))
    return attended.reshape(total_rows, heads_dev, head_dim)

def reference(queries, keys, values, decay_rates, norm_gain, out_weight, doc_lengths):
    doc_ends = jnp.cumsum(doc_lengths).astype(jnp.int32)
    positions = jnp.arange(TOKENS, dtype=jnp.int32)
    segments = lax.optimization_barrier(jnp.sum((doc_ends[None, :] <= positions[:, None]).astype(jnp.int32), axis=1)).astype(jnp.int32)
    shaped = (TOKENS, HEADS, HEAD_DIM)
    attended = local_pass(queries.astype(jnp.float32).reshape(shaped), keys.astype(jnp.float32).reshape(shaped), values.astype(jnp.float32).reshape(shaped), segments, decay_rates.astype(jnp.float32), jnp.array(-1, jnp.int32))
    flat = attended.reshape(TOKENS, HEADS * HEAD_DIM)
    power = lax.optimization_barrier(jnp.mean(flat * flat, axis=1))
    normed = (flat * lax.rsqrt(power + 1e-06)[:, None] * norm_gain[None, :]).astype(jnp.bfloat16)
    columns = HEADS * HEAD_DIM // N_TP
    mixed = jnp.zeros((TOKENS, D), jnp.float32)
    for group in range(N_TP):
        part = jnp.dot(normed[:, group * columns:(group + 1) * columns], out_weight[group * columns:(group + 1) * columns], preferred_element_type=jnp.float32).astype(jnp.bfloat16)
        mixed = mixed + part.astype(jnp.float32)
    return mixed.astype(jnp.bfloat16)
```

```python
import functools

import jax
import jax.numpy as jnp
from jax import lax
from jax.experimental import pallas as pl
from jax.experimental.pallas import tpu as pltpu
from jax.sharding import PartitionSpec as P


def carried_in(x, axis, combine, identity):
    count, position = (lax.axis_size(axis), lax.axis_index(axis))
    everything = jax.tree.map(
        lambda part, kind: lax.all_gather(part.astype(kind), axis), x, (jnp.bfloat16, jnp.bfloat16)
    )
    start = jax.tree.map(
        lambda part, zero: jnp.broadcast_to(jnp.asarray(zero, part.dtype), part.shape), x, identity
    )

    def step(k, before):
        reached = k < position
        new = combine(
            before, jax.tree.map(lambda part, own: part[k].astype(own.dtype), everything, x)
        )
        return jax.tree.map(lambda a, b: jnp.where(reached, a, b), new, before)

    return lax.fori_loop(0, count, step, start)


def segment_ids(positions, doc_ends):
    return jnp.sum((doc_ends[None, :] <= positions[:, None]).astype(jnp.int32), axis=1)


def local_pass(q_heads, k_heads, v_heads, segments, decay_rates, seg_start):
    highest = lax.Precision.HIGHEST
    total_rows, heads_dev, head_dim = q_heads.shape
    block_rows = min(256, total_rows)
    block_count = total_rows // block_rows
    shape_four = (block_count, block_rows, heads_dev, head_dim)
    q_blocks = q_heads.reshape(shape_four)
    k_blocks = k_heads.reshape(shape_four)
    v_blocks = v_heads.reshape(shape_four)
    seg_blocks = segments.reshape(block_count, block_rows)
    offsets = jnp.arange(block_rows).astype(jnp.float32)
    distance = offsets[:, None] - offsets[None, :]
    causal = distance >= 0
    base_decay = jnp.exp(-decay_rates[:, None, None] * jnp.maximum(distance, 0.0)[None])
    allowed = causal[None] & (seg_blocks[:, :, None] == seg_blocks[:, None, :])
    decay_mat = jnp.where(allowed[:, None], base_decay[None], 0.0)
    scores = jnp.einsum("bthd,bshd->bhts", q_blocks, k_blocks, preferred_element_type=jnp.float32)
    weighted = (scores * decay_mat).astype(jnp.bfloat16)
    inside = jnp.einsum("bhts,bshd->bthd", weighted, v_blocks, preferred_element_type=jnp.float32)
    last_segs = seg_blocks[:, -1]
    prev_segs = jnp.concatenate([jnp.reshape(seg_start, (1,)), last_segs[:-1]])
    carry_in = jnp.where(
        (seg_blocks == prev_segs[:, None])[:, :, None],
        jnp.exp(-decay_rates[None, :] * (offsets + 1.0)[:, None])[None],
        0.0,
    )
    keep_end = jnp.where(
        (seg_blocks == last_segs[:, None])[:, :, None],
        jnp.exp(-decay_rates[None, :] * (block_rows - 1.0 - offsets)[:, None])[None],
        0.0,
    )
    whole_keep = jnp.where(
        (last_segs == prev_segs)[:, None], jnp.exp(-decay_rates * block_rows)[None, :], 0.0
    )
    weighted_keys = (k_blocks.astype(jnp.float32) * keep_end[:, :, :, None]).astype(jnp.bfloat16)
    local_states = jnp.einsum(
        "bshd,bshe->bhde", weighted_keys, v_blocks, preferred_element_type=jnp.float32
    )

    def advance(running, pieces):
        kv_state, decay_total = running
        keep_now, state_now = pieces
        following = keep_now[:, None, None] * kv_state + state_now
        return ((following, decay_total * keep_now), kv_state)

    initial = (
        jnp.zeros((heads_dev, head_dim, head_dim), jnp.float32),
        jnp.ones((heads_dev,), jnp.float32),
    )
    finished, entering = lax.scan(advance, initial, (whole_keep, local_states))
    carried = jnp.einsum(
        "bthd,bhde->bthe", q_blocks.astype(jnp.float32), entering, precision=highest
    )
    attended = inside + carried * carry_in[:, :, :, None]
    return (attended.reshape(total_rows, heads_dev, head_dim), finished[0], finished[1])


def combine_states(earlier, later):
    return (earlier[0] * later[0], later[0][:, None, None] * earlier[1] + later[1])


def local(queries, keys, values, decay_rates, norm_gain, out_weight, doc_lengths):
    highest = lax.Precision.HIGHEST
    q_heads, k_heads, v_heads = (
        lax.all_to_all(queries, "tp", split_axis=1, concat_axis=0, tiled=True),
        lax.all_to_all(keys, "tp", split_axis=1, concat_axis=0, tiled=True),
        lax.all_to_all(values, "tp", split_axis=1, concat_axis=0, tiled=True),
    )
    heads_dev = decay_rates.shape[0]
    seq_rows = q_heads.shape[0]
    head_dim = q_heads.shape[1] // heads_dev
    group_size = lax.axis_size("tp")
    first_row = lax.axis_index("seq") * seq_rows
    doc_ends = jnp.cumsum(doc_lengths)
    positions = first_row + jnp.arange(seq_rows, dtype=jnp.int32)
    segments = segment_ids(positions, doc_ends)
    seg_before = segment_ids(jnp.reshape(first_row - 1, (1,)), doc_ends)[0]
    shaped = (seq_rows, heads_dev, head_dim)
    attended, kv_state, decay_total = local_pass(
        q_heads.reshape(shaped),
        k_heads.reshape(shaped),
        v_heads.reshape(shaped),
        segments,
        decay_rates,
        seg_before,
    )
    prefix = carried_in(
        (decay_total, kv_state),
        "seq",
        combine_states,
        (jnp.ones_like(decay_total), jnp.zeros_like(kv_state)),
    )
    incoming = prefix[1]
    steps_in = jnp.arange(seq_rows).astype(jnp.float32) + 1.0
    carry_in = jnp.where(
        (segments == seg_before)[None, :], jnp.exp(-decay_rates[:, None] * steps_in[None, :]), 0.0
    )
    wide_queries = q_heads.reshape(shaped).astype(jnp.float32)
    attended = (
        attended
        + jnp.einsum("thd,hde->the", wide_queries, incoming, precision=highest)
        * carry_in.T[:, :, None]
    )
    flat = attended.reshape(seq_rows, heads_dev * head_dim)
    power_sum = lax.psum(jnp.sum(flat * flat, axis=1), "tp")
    inv_rms = lax.rsqrt(power_sum / (heads_dev * head_dim * group_size) + 1e-06)
    normed = (flat * inv_rms[:, None] * norm_gain[None, :]).astype(jnp.bfloat16)
    return lax.psum_scatter(
        jnp.dot(normed, out_weight, preferred_element_type=jnp.float32)
        .astype(jnp.bfloat16)
        .astype(jnp.float32)
        .astype(jnp.bfloat16),
        "tp",
        scatter_dimension=0,
        tiled=True,
    )

MESH = pl.DeviceIdType.MESH
FAR = 1e12
BLOCK = 256
HEAD_CHUNKS = 4
COL_CHUNKS = 12


def layer_kernel(
    seq_count, rates, lengths, gain, q_in, k_in, v_in, w_in, out,
    qb, kb, vb, wb, ab, dist, dist_end, dist_in, states, chain_in, chain_out, power,
    pow_send, pow_recv, prod, first_in, second_out, second_in,
    a2a_send, a2a_recv, own_sem, w_sem, chain_send, chain_recv, pow_ss, pow_rs, fs, fr, ss, sr,
):
    seq, me = lax.axis_index("seq"), lax.axis_index("tp")
    x, y = lax.rem(me, 2), me // 2
    peers = (y * 2 + (1 - x), (1 - y) * 2 + x, (1 - y) * 2 + (1 - x))
    rows, width = q_in.shape[0], qb.shape[1]
    group_rows = qb.shape[0]
    heads = width // 128
    chunk_heads = heads // HEAD_CHUNKS
    chunk_cols = width // HEAD_CHUNKS
    out_cols = out.shape[1] // COL_CHUNKS
    blocks = group_rows // BLOCK
    tensors = ((k_in, kb), (v_in, vb), (q_in, qb))

    barrier = pltpu.get_barrier_semaphore()
    for peer in peers:
        pl.semaphore_signal(barrier, inc=1, device_id={"tp": peer}, device_id_type=MESH)

    @pl.when(seq > 0)
    def _():
        pl.semaphore_signal(barrier, inc=1, device_id={"seq": seq - 1}, device_id_type=MESH)

    @pl.when(seq < seq_count - 1)
    def _():
        pl.semaphore_signal(barrier, inc=1, device_id={"seq": seq + 1}, device_id_type=MESH)

    def own_copy(i):
        src, dst = tensors[i]
        cols = pl.ds(pl.multiple_of(me * width, 128), width)
        return pltpu.make_async_copy(
            src.at[:, cols], dst.at[pl.ds(pl.multiple_of(me * rows, 128), rows)], own_sem.at[i]
        )

    for i in range(3):
        own_copy(i).start()

    before, after = (seq + seq_count - 1) // seq_count, (2 * seq_count - 2 - seq) // seq_count
    pl.semaphore_wait(barrier, 3 + before + after)

    def exchange(i, c, d):
        src, dst = tensors[i]
        peer = peers[d]
        return pltpu.make_async_remote_copy(
            src_ref=src.at[:, pl.ds(pl.multiple_of(peer * width + c * chunk_cols, 128), chunk_cols)],
            dst_ref=dst.at[
                pl.ds(pl.multiple_of(me * rows, 128), rows),
                pl.ds(pl.multiple_of(c * chunk_cols, 128), chunk_cols),
            ],
            send_sem=a2a_send.at[i, c, d],
            recv_sem=a2a_recv.at[i, c, d],
            device_id={"tp": peer},
            device_id_type=MESH,
        )

    def send_kv(c, _):
        for i in (0, 1):
            for d in (2, 0, 1):
                exchange(i, c, d).start()
        return 0

    def send_q(c, _):
        for d in (2, 0, 1):
            exchange(2, c, d).start()
        return 0

    lax.fori_loop(0, HEAD_CHUNKS, send_kv, 0)
    lax.fori_loop(0, HEAD_CHUNKS, send_q, 0)
    load_w = pltpu.make_async_copy(w_in, wb, w_sem)
    load_w.start()

    first_row = seq * group_rows
    ends, end = [], jnp.int32(0)
    for j in range(lengths.shape[0]):
        end = end + lengths[j]
        ends.append(end)

    def scalar_seg(position):
        seg = jnp.int32(0)
        for e in ends:
            seg = seg + jnp.where(e <= position, 1, 0)
        return seg

    edge_segs = [scalar_seg(first_row - 1 + b * BLOCK) for b in range(blocks + 1)]
    for b in range(blocks):
        base = first_row + b * BLOCK
        pos_c = lax.broadcasted_iota(jnp.int32, (BLOCK, 128), 0)
        pos_r = lax.broadcasted_iota(jnp.int32, (8, BLOCK), 1)
        seg_c, seg_r = jnp.zeros_like(pos_c), jnp.zeros_like(pos_r)
        for e in ends:
            seg_c = seg_c + jnp.where(e - base <= pos_c, 1, 0)
            seg_r = seg_r + jnp.where(e - base <= pos_r, 1, 0)
        steps = pos_c.astype(jnp.float32)
        dist_end[b] = jnp.where(seg_c == edge_segs[b + 1], BLOCK - 1.0 - steps, FAR)
        dist_in[b] = jnp.where(seg_c == edge_segs[b], steps + 1.0, FAR)
        ti = lax.broadcasted_iota(jnp.int32, (BLOCK, BLOCK), 0)
        si = lax.broadcasted_iota(jnp.int32, (BLOCK, BLOCK), 1)
        same = jnp.concatenate([seg_c] * (BLOCK // 128), axis=1) == jnp.broadcast_to(
            seg_r[:1], (BLOCK, BLOCK)
        )
        dist[b] = jnp.where(same & (ti >= si), (ti - si).astype(jnp.float32), FAR)
    keep_dist = [
        jnp.where(edge_segs[b + 1] == edge_segs[b], jnp.float32(BLOCK), jnp.float32(FAR))
        for b in range(blocks)
    ]

    @pl.when(seq == 0)
    def _():
        chain_in[...] = jnp.zeros_like(chain_in)

    def hop(c):
        return pltpu.make_async_remote_copy(
            src_ref=chain_out.at[c],
            dst_ref=chain_in.at[c],
            send_sem=chain_send.at[c],
            recv_sem=chain_recv.at[c],
            device_id={"seq": lax.rem(seq + 1, seq_count)},
            device_id_type=MESH,
        )

    own_copy(0).wait()
    own_copy(1).wait()

    def state_chunk(c, _):
        for i in (0, 1):
            for d in range(3):
                exchange(i, c, d).wait_recv()
        for g in range(chunk_heads):
            h = c * chunk_heads + g
            cols = pl.ds(pl.multiple_of(h * 128, 128), 128)
            rate = rates[h]
            for b in range(blocks):
                span = pl.ds(b * BLOCK, BLOCK)
                weight = jnp.exp(dist_end[b] * -rate)
                wk = (kb[span, cols].astype(jnp.float32) * weight).astype(jnp.bfloat16)
                states[b, h] = lax.dot_general(
                    wk, vb[span, cols], (((0,), (0,)), ((), ())), preferred_element_type=jnp.float32
                )

        @pl.when(seq > 0)
        def _():
            hop(c).wait_recv()

        for g in range(chunk_heads):
            h = c * chunk_heads + g
            rate = rates[h]
            entering = chain_in[c, g].astype(jnp.float32)
            for b in range(blocks):
                keep = jnp.exp(jnp.full((128, 128), keep_dist[b] * -rate, jnp.float32))
                following = keep * entering + states[b, h]
                states[b, h] = entering
                entering = following
            chain_out[c, g] = entering.astype(jnp.bfloat16)

        @pl.when(seq < seq_count - 1)
        def _():
            hop(c).start()

        return 0

    lax.fori_loop(0, HEAD_CHUNKS, state_chunk, 0)

    power[...] = jnp.zeros_like(power)
    own_copy(2).wait()

    def attend_chunk(c, _):
        for d in range(3):
            exchange(2, c, d).wait_recv()
        for g in range(chunk_heads):
            h = c * chunk_heads + g
            cols = pl.ds(pl.multiple_of(h * 128, 128), 128)
            rate = rates[h]
            for b in range(blocks):
                span = pl.ds(b * BLOCK, BLOCK)
                q, k, v = qb[span, cols], kb[span, cols], vb[span, cols]
                scores = lax.dot_general(
                    q, k, (((1,), (1,)), ((), ())), preferred_element_type=jnp.float32
                )
                weighted = (scores * jnp.exp(dist[b] * -rate)).astype(jnp.bfloat16)
                inside = jnp.dot(weighted, v, preferred_element_type=jnp.float32)
                carried = jnp.dot(
                    q, states[b, h].astype(jnp.bfloat16), preferred_element_type=jnp.float32
                )
                attended = inside + carried * jnp.exp(dist_in[b] * -rate)
                power[span] += attended * attended
                ab[span, cols] = (attended * gain[:, cols]).astype(jnp.bfloat16)
        return 0

    lax.fori_loop(0, HEAD_CHUNKS, attend_chunk, 0)
    load_w.wait()

    def ways(c):
        odd = lax.rem(c, 2)
        p1 = peers[0] * (1 - odd) + peers[1] * odd
        p2 = peers[1] * (1 - odd) + peers[0] * odd
        return p1, p2

    def first_hop(c, which):
        p1, _ = ways(c)
        return pltpu.make_async_remote_copy(
            src_ref=prod.at[c, p1 if which == 0 else peers[2]],
            dst_ref=first_in.at[c, which],
            send_sem=fs.at[c, which],
            recv_sem=fr.at[c, which],
            device_id={"tp": p1},
            device_id_type=MESH,
        )

    def second_hop(c):
        _, p2 = ways(c)
        return pltpu.make_async_remote_copy(
            src_ref=second_out.at[c],
            dst_ref=second_in.at[c],
            send_sem=ss.at[c],
            recv_sem=sr.at[c],
            device_id={"tp": p2},
            device_id_type=MESH,
        )

    def pow_copy(d):
        return pltpu.make_async_remote_copy(
            src_ref=pow_send.at[peers[d]],
            dst_ref=pow_recv.at[d],
            send_sem=pow_ss.at[d],
            recv_sem=pow_rs.at[d],
            device_id={"tp": peers[d]},
            device_id_type=MESH,
        )

    def project(c):
        cols = pl.ds(pl.multiple_of(c * out_cols, 128), out_cols)
        part = jnp.dot(ab[...], wb[:, cols], preferred_element_type=jnp.float32)
        prod[c] = part.astype(jnp.bfloat16).reshape(prod.shape[1:])
        first_hop(c, 1).start()
        first_hop(c, 0).start()

    def forward(c):
        _, p2 = ways(c)
        first_hop(c, 1).wait_recv()
        second_out[c] = (
            prod[c, p2].astype(jnp.float32) + first_in[c, 1].astype(jnp.float32)
        ).astype(jnp.bfloat16)
        second_hop(c).start()

    lag = 3

    def lead(c, _):
        project(c)
        return 0

    def steady(c, _):
        project(c)
        forward(c - lag)
        return 0

    def trail(c, _):
        forward(c)
        return 0

    lax.fori_loop(0, lag, lead, 0)
    for j in range(4):
        row = jnp.sum(power[pl.ds(j * rows, rows)].T, axis=0, keepdims=True)
        pow_send[j] = jnp.broadcast_to(row, pow_send.shape[1:])
    for d in range(3):
        pow_copy(d).start()
    lax.fori_loop(lag, COL_CHUNKS, steady, 0)
    lax.fori_loop(COL_CHUNKS - lag, COL_CHUNKS, trail, 0)

    total = pow_send[me]
    for d in range(3):
        pow_copy(d).wait_recv()
        total = total + pow_recv[d]
    scale = lax.rsqrt(total / (4 * width) + 1e-06)
    scale = jnp.broadcast_to(scale[:1], (128, rows)).T
    scale = jnp.concatenate([scale] * (out_cols // 128), axis=1)

    def finish(c, _):
        first_hop(c, 0).wait_recv()
        second_hop(c).wait_recv()
        summed = (
            prod[c, me].astype(jnp.float32)
            + first_in[c, 0].astype(jnp.float32)
            + second_in[c].astype(jnp.float32)
        )
        cols = pl.ds(pl.multiple_of(c * out_cols, 128), out_cols)
        out[:, cols] = (summed * scale).astype(jnp.bfloat16)
        return 0

    lax.fori_loop(0, COL_CHUNKS, finish, 0)

    def drain_heads(c, _):
        for i in range(3):
            for d in range(3):
                exchange(i, c, d).wait_send()

        @pl.when(seq < seq_count - 1)
        def _():
            hop(c).wait_send()

        return 0

    def drain_cols(c, _):
        first_hop(c, 0).wait_send()
        first_hop(c, 1).wait_send()
        second_hop(c).wait_send()
        return 0

    lax.fori_loop(0, HEAD_CHUNKS, drain_heads, 0)
    lax.fori_loop(0, COL_CHUNKS, drain_cols, 0)
    for d in range(3):
        pow_copy(d).wait_send()


def fused(queries, keys, values, decay_rates, norm_gain, out_weight, doc_lengths):
    rows, model = queries.shape
    width, out_width = out_weight.shape
    heads = width // 128
    group = rows * 4
    blocks = group // BLOCK
    per = heads // HEAD_CHUNKS
    cols = out_width // COL_CHUNKS
    bf16, f32 = jnp.bfloat16, jnp.float32
    hbm, vmem = pl.BlockSpec(memory_space=pl.ANY), pl.BlockSpec(memory_space=pltpu.VMEM)
    smem = pl.BlockSpec(memory_space=pltpu.SMEM)
    dma = pltpu.SemaphoreType.DMA
    return pl.pallas_call(
        functools.partial(layer_kernel, lax.axis_size("seq")),
        out_shape=jax.ShapeDtypeStruct((rows, out_width), bf16),
        in_specs=[smem, smem, vmem, hbm, hbm, hbm, hbm],
        out_specs=vmem,
        scratch_shapes=[
            pltpu.VMEM((group, width), bf16),
            pltpu.VMEM((group, width), bf16),
            pltpu.VMEM((group, width), bf16),
            pltpu.VMEM((width, out_width), bf16),
            pltpu.VMEM((group, width), bf16),
            pltpu.VMEM((blocks, BLOCK, BLOCK), f32),
            pltpu.VMEM((blocks, BLOCK, 128), f32),
            pltpu.VMEM((blocks, BLOCK, 128), f32),
            pltpu.VMEM((blocks, heads, 128, 128), f32),
            pltpu.VMEM((HEAD_CHUNKS, per, 128, 128), bf16),
            pltpu.VMEM((HEAD_CHUNKS, per, 128, 128), bf16),
            pltpu.VMEM((group, 128), f32),
            pltpu.VMEM((4, 8, rows), f32),
            pltpu.VMEM((3, 8, rows), f32),
            pltpu.VMEM((COL_CHUNKS, 4, rows, cols), bf16),
            pltpu.VMEM((COL_CHUNKS, 2, rows, cols), bf16),
            pltpu.VMEM((COL_CHUNKS, rows, cols), bf16),
            pltpu.VMEM((COL_CHUNKS, rows, cols), bf16),
            dma((3, HEAD_CHUNKS, 3)),
            dma((3, HEAD_CHUNKS, 3)),
            dma((3,)),
            dma,
            dma((HEAD_CHUNKS,)),
            dma((HEAD_CHUNKS,)),
            dma((3,)),
            dma((3,)),
            dma((COL_CHUNKS, 2)),
            dma((COL_CHUNKS, 2)),
            dma((COL_CHUNKS,)),
            dma((COL_CHUNKS,)),
        ],
        compiler_params=pltpu.CompilerParams(
            collective_id=0, has_side_effects=True, vmem_limit_bytes=58 * 2**20
        ),
        name="layer",
    )(decay_rates, doc_lengths, norm_gain.reshape(1, width), queries, keys, values, out_weight)


def solution(mesh):
    return jax.shard_map(
        fused if mesh.shape["tp"] == 4 else local,
        mesh=mesh,
        in_specs=(
            P(("seq", "tp"), None),
            P(("seq", "tp"), None),
            P(("seq", "tp"), None),
            P("tp"),
            P("tp"),
            P("tp", None),
            P(),
        ),
        out_specs=P(("seq", "tp"), None),
        check_vma=False,
    )
```

```python
import functools

import jax
import jax.numpy as jnp
from jax import lax
from jax.experimental import pallas as pl
from jax.experimental.pallas import tpu as pltpu
from jax.sharding import PartitionSpec as P


def carried_in(x, axis, combine, identity):
    count, position = (lax.axis_size(axis), lax.axis_index(axis))
    everything = jax.tree.map(
        lambda part, kind: lax.all_gather(part.astype(kind), axis), x, (jnp.bfloat16, jnp.bfloat16)
    )
    start = jax.tree.map(
        lambda part, zero: jnp.broadcast_to(jnp.asarray(zero, part.dtype), part.shape), x, identity
    )

    def step(k, before):
        reached = k < position
        new = combine(
            before, jax.tree.map(lambda part, own: part[k].astype(own.dtype), everything, x)
        )
        return jax.tree.map(lambda a, b: jnp.where(reached, a, b), new, before)

    return lax.fori_loop(0, count, step, start)


def segment_ids(positions, doc_ends):
    return jnp.sum((doc_ends[None, :] <= positions[:, None]).astype(jnp.int32), axis=1)


def local_pass(q_heads, k_heads, v_heads, segments, decay_rates, seg_start):
    highest = lax.Precision.HIGHEST
    total_rows, heads_dev, head_dim = q_heads.shape
    block_rows = min(256, total_rows)
    block_count = total_rows // block_rows
    shape_four = (block_count, block_rows, heads_dev, head_dim)
    q_blocks = q_heads.reshape(shape_four)
    k_blocks = k_heads.reshape(shape_four)
    v_blocks = v_heads.reshape(shape_four)
    seg_blocks = segments.reshape(block_count, block_rows)
    offsets = jnp.arange(block_rows).astype(jnp.float32)
    distance = offsets[:, None] - offsets[None, :]
    causal = distance >= 0
    base_decay = jnp.exp(-decay_rates[:, None, None] * jnp.maximum(distance, 0.0)[None])
    allowed = causal[None] & (seg_blocks[:, :, None] == seg_blocks[:, None, :])
    decay_mat = jnp.where(allowed[:, None], base_decay[None], 0.0)
    scores = jnp.einsum("bthd,bshd->bhts", q_blocks, k_blocks, preferred_element_type=jnp.float32)
    weighted = (scores * decay_mat).astype(jnp.bfloat16)
    inside = jnp.einsum("bhts,bshd->bthd", weighted, v_blocks, preferred_element_type=jnp.float32)
    last_segs = seg_blocks[:, -1]
    prev_segs = jnp.concatenate([jnp.reshape(seg_start, (1,)), last_segs[:-1]])
    carry_in = jnp.where(
        (seg_blocks == prev_segs[:, None])[:, :, None],
        jnp.exp(-decay_rates[None, :] * (offsets + 1.0)[:, None])[None],
        0.0,
    )
    keep_end = jnp.where(
        (seg_blocks == last_segs[:, None])[:, :, None],
        jnp.exp(-decay_rates[None, :] * (block_rows - 1.0 - offsets)[:, None])[None],
        0.0,
    )
    whole_keep = jnp.where(
        (last_segs == prev_segs)[:, None], jnp.exp(-decay_rates * block_rows)[None, :], 0.0
    )
    weighted_keys = (k_blocks.astype(jnp.float32) * keep_end[:, :, :, None]).astype(jnp.bfloat16)
    local_states = jnp.einsum(
        "bshd,bshe->bhde", weighted_keys, v_blocks, preferred_element_type=jnp.float32
    )

    def advance(running, pieces):
        kv_state, decay_total = running
        keep_now, state_now = pieces
        following = keep_now[:, None, None] * kv_state + state_now
        return ((following, decay_total * keep_now), kv_state)

    initial = (
        jnp.zeros((heads_dev, head_dim, head_dim), jnp.float32),
        jnp.ones((heads_dev,), jnp.float32),
    )
    finished, entering = lax.scan(advance, initial, (whole_keep, local_states))
    carried = jnp.einsum(
        "bthd,bhde->bthe", q_blocks.astype(jnp.float32), entering, precision=highest
    )
    attended = inside + carried * carry_in[:, :, :, None]
    return (attended.reshape(total_rows, heads_dev, head_dim), finished[0], finished[1])


def combine_states(earlier, later):
    return (earlier[0] * later[0], later[0][:, None, None] * earlier[1] + later[1])


def local(queries, keys, values, decay_rates, norm_gain, out_weight, doc_lengths):
    highest = lax.Precision.HIGHEST
    q_heads, k_heads, v_heads = (
        lax.all_to_all(queries, "tp", split_axis=1, concat_axis=0, tiled=True),
        lax.all_to_all(keys, "tp", split_axis=1, concat_axis=0, tiled=True),
        lax.all_to_all(values, "tp", split_axis=1, concat_axis=0, tiled=True),
    )
    heads_dev = decay_rates.shape[0]
    seq_rows = q_heads.shape[0]
    head_dim = q_heads.shape[1] // heads_dev
    group_size = lax.axis_size("tp")
    first_row = lax.axis_index("seq") * seq_rows
    doc_ends = jnp.cumsum(doc_lengths)
    positions = first_row + jnp.arange(seq_rows, dtype=jnp.int32)
    segments = segment_ids(positions, doc_ends)
    seg_before = segment_ids(jnp.reshape(first_row - 1, (1,)), doc_ends)[0]
    shaped = (seq_rows, heads_dev, head_dim)
    attended, kv_state, decay_total = local_pass(
        q_heads.reshape(shaped),
        k_heads.reshape(shaped),
        v_heads.reshape(shaped),
        segments,
        decay_rates,
        seg_before,
    )
    prefix = carried_in(
        (decay_total, kv_state),
        "seq",
        combine_states,
        (jnp.ones_like(decay_total), jnp.zeros_like(kv_state)),
    )
    incoming = prefix[1]
    steps_in = jnp.arange(seq_rows).astype(jnp.float32) + 1.0
    carry_in = jnp.where(
        (segments == seg_before)[None, :], jnp.exp(-decay_rates[:, None] * steps_in[None, :]), 0.0
    )
    wide_queries = q_heads.reshape(shaped).astype(jnp.float32)
    attended = (
        attended
        + jnp.einsum("thd,hde->the", wide_queries, incoming, precision=highest)
        * carry_in.T[:, :, None]
    )
    flat = attended.reshape(seq_rows, heads_dev * head_dim)
    power_sum = lax.psum(jnp.sum(flat * flat, axis=1), "tp")
    inv_rms = lax.rsqrt(power_sum / (heads_dev * head_dim * group_size) + 1e-06)
    normed = (flat * inv_rms[:, None] * norm_gain[None, :]).astype(jnp.bfloat16)
    return lax.psum_scatter(
        jnp.dot(normed, out_weight, preferred_element_type=jnp.float32)
        .astype(jnp.bfloat16)
        .astype(jnp.float32)
        .astype(jnp.bfloat16),
        "tp",
        scatter_dimension=0,
        tiled=True,
    )

MESH = pl.DeviceIdType.MESH
FAR = 1e12
BLOCK = 256
HEAD_CHUNKS = 4
COL_CHUNKS = 12
LAG = 4


def layer_kernel(
    seq_count, rates, lengths, gain, q_in, k_in, v_in, w_in, out,
    qb, kb, vb, wb, ab, dist, dist_end, dist_in, states, chain_in, chain_out, power,
    pow_send, pow_recv, prod, first_in, second_out, second_in,
    a2a_send, a2a_recv, own_sem, w_sem, chain_send, chain_recv, pow_ss, pow_rs, fs, fr, ss, sr,
):
    seq, me = lax.axis_index("seq"), lax.axis_index("tp")
    x, y = lax.rem(me, 2), me // 2
    peers = (y * 2 + (1 - x), (1 - y) * 2 + x, (1 - y) * 2 + (1 - x))
    rows, width = q_in.shape[0], qb.shape[1]
    group_rows = qb.shape[0]
    heads = width // 128
    chunk_heads = heads // HEAD_CHUNKS
    chunk_cols = width // HEAD_CHUNKS
    out_cols = out.shape[1] // COL_CHUNKS
    blocks = group_rows // BLOCK
    tensors = ((k_in, kb), (v_in, vb), (q_in, qb))

    barrier = pltpu.get_barrier_semaphore()
    for peer in peers:
        pl.semaphore_signal(barrier, inc=1, device_id={"tp": peer}, device_id_type=MESH)

    @pl.when(seq > 0)
    def _():
        pl.semaphore_signal(barrier, inc=1, device_id={"seq": seq - 1}, device_id_type=MESH)

    @pl.when(seq < seq_count - 1)
    def _():
        pl.semaphore_signal(barrier, inc=1, device_id={"seq": seq + 1}, device_id_type=MESH)

    def own_copy(i):
        src, dst = tensors[i]
        cols = pl.ds(pl.multiple_of(me * width, 128), width)
        return pltpu.make_async_copy(
            src.at[:, cols], dst.at[pl.ds(pl.multiple_of(me * rows, 128), rows)], own_sem.at[i]
        )

    for i in range(3):
        own_copy(i).start()

    before, after = (seq + seq_count - 1) // seq_count, (2 * seq_count - 2 - seq) // seq_count
    pl.semaphore_wait(barrier, 3 + before + after)

    def exchange(i, c, d):
        src, dst = tensors[i]
        peer = peers[d]
        return pltpu.make_async_remote_copy(
            src_ref=src.at[:, pl.ds(pl.multiple_of(peer * width + c * chunk_cols, 128), chunk_cols)],
            dst_ref=dst.at[
                pl.ds(pl.multiple_of(me * rows, 128), rows),
                pl.ds(pl.multiple_of(c * chunk_cols, 128), chunk_cols),
            ],
            send_sem=a2a_send.at[i, c, d],
            recv_sem=a2a_recv.at[i, c, d],
            device_id={"tp": peer},
            device_id_type=MESH,
        )

    def send_kv(c, _):
        for i in (0, 1):
            for d in (2, 0, 1):
                exchange(i, c, d).start()
        return 0

    def send_q(c, _):
        for d in (2, 0, 1):
            exchange(2, c, d).start()
        return 0

    lax.fori_loop(0, HEAD_CHUNKS, send_kv, 0)
    lax.fori_loop(0, HEAD_CHUNKS, send_q, 0)
    load_w = pltpu.make_async_copy(w_in, wb, w_sem)
    load_w.start()

    first_row = seq * group_rows
    ends, end = [], jnp.int32(0)
    for j in range(lengths.shape[0]):
        end = end + lengths[j]
        ends.append(end)

    def scalar_seg(position):
        seg = jnp.int32(0)
        for e in ends:
            seg = seg + jnp.where(e <= position, 1, 0)
        return seg

    edge_segs = [scalar_seg(first_row - 1 + b * BLOCK) for b in range(blocks + 1)]
    for b in range(blocks):
        base = first_row + b * BLOCK
        pos_c = lax.broadcasted_iota(jnp.int32, (BLOCK, 128), 0)
        pos_r = lax.broadcasted_iota(jnp.int32, (8, BLOCK), 1)
        seg_c, seg_r = jnp.zeros_like(pos_c), jnp.zeros_like(pos_r)
        for e in ends:
            seg_c = seg_c + jnp.where(e - base <= pos_c, 1, 0)
            seg_r = seg_r + jnp.where(e - base <= pos_r, 1, 0)
        steps = pos_c.astype(jnp.float32)
        dist_end[b] = jnp.where(seg_c == edge_segs[b + 1], BLOCK - 1.0 - steps, FAR)
        dist_in[b] = jnp.where(seg_c == edge_segs[b], steps + 1.0, FAR)
        ti = lax.broadcasted_iota(jnp.int32, (BLOCK, BLOCK), 0)
        si = lax.broadcasted_iota(jnp.int32, (BLOCK, BLOCK), 1)
        same = jnp.concatenate([seg_c] * (BLOCK // 128), axis=1) == jnp.broadcast_to(
            seg_r[:1], (BLOCK, BLOCK)
        )
        dist[b] = jnp.where(same & (ti >= si), (ti - si).astype(jnp.float32), FAR)
    keep_dist = [
        jnp.where(edge_segs[b + 1] == edge_segs[b], jnp.float32(BLOCK), jnp.float32(FAR))
        for b in range(blocks)
    ]

    @pl.when(seq == 0)
    def _():
        chain_in[...] = jnp.zeros_like(chain_in)

    def hop(c):
        return pltpu.make_async_remote_copy(
            src_ref=chain_out.at[c],
            dst_ref=chain_in.at[c],
            send_sem=chain_send.at[c],
            recv_sem=chain_recv.at[c],
            device_id={"seq": lax.rem(seq + 1, seq_count)},
            device_id_type=MESH,
        )

    own_copy(0).wait()
    own_copy(1).wait()

    def state_chunk(c, _):
        for i in (0, 1):
            for d in range(3):
                exchange(i, c, d).wait_recv()
        for g in range(chunk_heads):
            h = c * chunk_heads + g
            cols = pl.ds(pl.multiple_of(h * 128, 128), 128)
            rate = rates[h]
            for b in range(blocks):
                span = pl.ds(b * BLOCK, BLOCK)
                weight = jnp.exp(dist_end[b] * -rate)
                wk = (kb[span, cols].astype(jnp.float32) * weight).astype(jnp.bfloat16)
                states[b, h] = lax.dot_general(
                    wk, vb[span, cols], (((0,), (0,)), ((), ())), preferred_element_type=jnp.float32
                )

        @pl.when(seq > 0)
        def _():
            hop(c).wait_recv()

        for g in range(chunk_heads):
            h = c * chunk_heads + g
            rate = rates[h]
            entering = chain_in[c, g].astype(jnp.float32)
            for b in range(blocks):
                keep = jnp.exp(jnp.full((128, 128), keep_dist[b] * -rate, jnp.float32))
                following = keep * entering + states[b, h]
                states[b, h] = entering
                entering = following
            chain_out[c, g] = entering.astype(jnp.bfloat16)

        @pl.when(seq < seq_count - 1)
        def _():
            hop(c).start()

        return 0

    lax.fori_loop(0, HEAD_CHUNKS, state_chunk, 0)

    power[...] = jnp.zeros_like(power)
    own_copy(2).wait()

    def attend_chunk(c, _):
        for d in range(3):
            exchange(2, c, d).wait_recv()
        for g in range(chunk_heads):
            h = c * chunk_heads + g
            cols = pl.ds(pl.multiple_of(h * 128, 128), 128)
            rate = rates[h]
            for b in range(blocks):
                span = pl.ds(b * BLOCK, BLOCK)
                q, k, v = qb[span, cols], kb[span, cols], vb[span, cols]
                scores = lax.dot_general(
                    q, k, (((1,), (1,)), ((), ())), preferred_element_type=jnp.float32
                )
                weighted = (scores * jnp.exp(dist[b] * -rate)).astype(jnp.bfloat16)
                inside = jnp.dot(weighted, v, preferred_element_type=jnp.float32)
                carried = jnp.dot(
                    q, states[b, h].astype(jnp.bfloat16), preferred_element_type=jnp.float32
                )
                attended = inside + carried * jnp.exp(dist_in[b] * -rate)
                power[span] += attended * attended
                ab[span, cols] = (attended * gain[cols]).astype(jnp.bfloat16)
        return 0

    lax.fori_loop(0, HEAD_CHUNKS, attend_chunk, 0)
    load_w.wait()

    def ways(c):
        odd = lax.rem(c, 2)
        p1 = peers[0] * (1 - odd) + peers[1] * odd
        p2 = peers[1] * (1 - odd) + peers[0] * odd
        return p1, p2

    def first_hop(c, which):
        p1, _ = ways(c)
        return pltpu.make_async_remote_copy(
            src_ref=prod.at[c, p1 if which == 0 else peers[2]],
            dst_ref=first_in.at[c, which],
            send_sem=fs.at[c, which],
            recv_sem=fr.at[c, which],
            device_id={"tp": p1},
            device_id_type=MESH,
        )

    def second_hop(c):
        _, p2 = ways(c)
        return pltpu.make_async_remote_copy(
            src_ref=second_out.at[c],
            dst_ref=second_in.at[c],
            send_sem=ss.at[c],
            recv_sem=sr.at[c],
            device_id={"tp": p2},
            device_id_type=MESH,
        )

    def pow_copy(d):
        return pltpu.make_async_remote_copy(
            src_ref=pow_send.at[peers[d]],
            dst_ref=pow_recv.at[d],
            send_sem=pow_ss.at[d],
            recv_sem=pow_rs.at[d],
            device_id={"tp": peers[d]},
            device_id_type=MESH,
        )

    def project(c):
        cols = pl.ds(pl.multiple_of(c * out_cols, 128), out_cols)
        part = jnp.dot(ab[...], wb[:, cols], preferred_element_type=jnp.float32)
        prod[c] = part.astype(jnp.bfloat16).reshape(prod.shape[1:])
        first_hop(c, 1).start()

    def forward(c):
        _, p2 = ways(c)
        first_hop(c, 1).wait_recv()
        second_out[c] = (
            prod[c, p2].astype(jnp.float32) + first_in[c, 1].astype(jnp.float32)
        ).astype(jnp.bfloat16)
        second_hop(c).start()
        first_hop(c, 0).start()

    lag = LAG

    def lead(c, _):
        project(c)
        return 0

    def steady(c, _):
        project(c)
        forward(c - lag)
        return 0

    def trail(c, _):
        forward(c)
        return 0

    lax.fori_loop(0, lag, lead, 0)
    for j in range(4):
        row = jnp.sum(power[pl.ds(j * rows, rows)].T, axis=0, keepdims=True)
        pow_send[j] = jnp.broadcast_to(row, pow_send.shape[1:])
    for d in range(3):
        pow_copy(d).start()
    lax.fori_loop(lag, COL_CHUNKS, steady, 0)
    lax.fori_loop(COL_CHUNKS - lag, COL_CHUNKS, trail, 0)

    total = pow_send[me]
    for d in range(3):
        pow_copy(d).wait_recv()
        total = total + pow_recv[d]
    scale = lax.rsqrt(total / (4 * width) + 1e-06)
    scale = jnp.broadcast_to(scale[:1], (128, rows)).T
    scale = jnp.concatenate([scale] * (out_cols // 128), axis=1)

    def finish(c, _):
        first_hop(c, 0).wait_recv()
        second_hop(c).wait_recv()
        summed = (
            prod[c, me].astype(jnp.float32)
            + first_in[c, 0].astype(jnp.float32)
            + second_in[c].astype(jnp.float32)
        )
        cols = pl.ds(pl.multiple_of(c * out_cols, 128), out_cols)
        out[:, cols] = (summed * scale).astype(jnp.bfloat16)
        return 0

    lax.fori_loop(0, COL_CHUNKS, finish, 0)

    def drain_heads(c, _):
        for i in range(3):
            for d in range(3):
                exchange(i, c, d).wait_send()

        @pl.when(seq < seq_count - 1)
        def _():
            hop(c).wait_send()

        return 0

    def drain_cols(c, _):
        first_hop(c, 0).wait_send()
        first_hop(c, 1).wait_send()
        second_hop(c).wait_send()
        return 0

    lax.fori_loop(0, HEAD_CHUNKS, drain_heads, 0)
    lax.fori_loop(0, COL_CHUNKS, drain_cols, 0)
    for d in range(3):
        pow_copy(d).wait_send()


def fused(queries, keys, values, decay_rates, norm_gain, out_weight, doc_lengths):
    rows, model = queries.shape
    width, out_width = out_weight.shape
    heads = width // 128
    group = rows * 4
    blocks = group // BLOCK
    per = heads // HEAD_CHUNKS
    cols = out_width // COL_CHUNKS
    bf16, f32 = jnp.bfloat16, jnp.float32
    hbm, vmem = pl.BlockSpec(memory_space=pl.ANY), pl.BlockSpec(memory_space=pltpu.VMEM)
    smem = pl.BlockSpec(memory_space=pltpu.SMEM)
    dma = pltpu.SemaphoreType.DMA
    return pl.pallas_call(
        functools.partial(layer_kernel, lax.axis_size("seq")),
        out_shape=jax.ShapeDtypeStruct((rows, out_width), bf16),
        in_specs=[smem, smem, vmem, hbm, hbm, hbm, hbm],
        out_specs=vmem,
        scratch_shapes=[
            pltpu.VMEM((group, width), bf16),
            pltpu.VMEM((group, width), bf16),
            pltpu.VMEM((group, width), bf16),
            pltpu.VMEM((width, out_width), bf16),
            pltpu.VMEM((group, width), bf16),
            pltpu.VMEM((blocks, BLOCK, BLOCK), f32),
            pltpu.VMEM((blocks, BLOCK, 128), f32),
            pltpu.VMEM((blocks, BLOCK, 128), f32),
            pltpu.VMEM((blocks, heads, 128, 128), f32),
            pltpu.VMEM((HEAD_CHUNKS, per, 128, 128), bf16),
            pltpu.VMEM((HEAD_CHUNKS, per, 128, 128), bf16),
            pltpu.VMEM((group, 128), f32),
            pltpu.VMEM((4, 8, rows), f32),
            pltpu.VMEM((3, 8, rows), f32),
            pltpu.VMEM((COL_CHUNKS, 4, rows, cols), bf16),
            pltpu.VMEM((COL_CHUNKS, 2, rows, cols), bf16),
            pltpu.VMEM((COL_CHUNKS, rows, cols), bf16),
            pltpu.VMEM((COL_CHUNKS, rows, cols), bf16),
            dma((3, HEAD_CHUNKS, 3)),
            dma((3, HEAD_CHUNKS, 3)),
            dma((3,)),
            dma,
            dma((HEAD_CHUNKS,)),
            dma((HEAD_CHUNKS,)),
            dma((3,)),
            dma((3,)),
            dma((COL_CHUNKS, 2)),
            dma((COL_CHUNKS, 2)),
            dma((COL_CHUNKS,)),
            dma((COL_CHUNKS,)),
        ],
        compiler_params=pltpu.CompilerParams(
            collective_id=0, has_side_effects=True, vmem_limit_bytes=58 * 2**20
        ),
        name="layer",
    )(decay_rates, doc_lengths, norm_gain, queries, keys, values, out_weight)


def solution(mesh):
    return jax.shard_map(
        fused if mesh.shape["tp"] == 4 else local,
        mesh=mesh,
        in_specs=(
            P(("seq", "tp"), None),
            P(("seq", "tp"), None),
            P(("seq", "tp"), None),
            P("tp"),
            P("tp"),
            P("tp", None),
            P(),
        ),
        out_specs=P(("seq", "tp"), None),
        check_vma=False,
    )
```

```python
import functools

import jax
import jax.numpy as jnp
from jax import lax
from jax.experimental import pallas as pl
from jax.experimental.pallas import tpu as pltpu
from jax.sharding import PartitionSpec as P


def carried_in(x, axis, combine, identity):
    count, position = (lax.axis_size(axis), lax.axis_index(axis))
    everything = jax.tree.map(
        lambda part, kind: lax.all_gather(part.astype(kind), axis), x, (jnp.bfloat16, jnp.bfloat16)
    )
    start = jax.tree.map(
        lambda part, zero: jnp.broadcast_to(jnp.asarray(zero, part.dtype), part.shape), x, identity
    )

    def step(k, before):
        reached = k < position
        new = combine(
            before, jax.tree.map(lambda part, own: part[k].astype(own.dtype), everything, x)
        )
        return jax.tree.map(lambda a, b: jnp.where(reached, a, b), new, before)

    return lax.fori_loop(0, count, step, start)


def segment_ids(positions, doc_ends):
    return jnp.sum((doc_ends[None, :] <= positions[:, None]).astype(jnp.int32), axis=1)


def local_pass(q_heads, k_heads, v_heads, segments, decay_rates, seg_start):
    highest = lax.Precision.HIGHEST
    total_rows, heads_dev, head_dim = q_heads.shape
    block_rows = min(256, total_rows)
    block_count = total_rows // block_rows
    shape_four = (block_count, block_rows, heads_dev, head_dim)
    q_blocks = q_heads.reshape(shape_four)
    k_blocks = k_heads.reshape(shape_four)
    v_blocks = v_heads.reshape(shape_four)
    seg_blocks = segments.reshape(block_count, block_rows)
    offsets = jnp.arange(block_rows).astype(jnp.float32)
    distance = offsets[:, None] - offsets[None, :]
    causal = distance >= 0
    base_decay = jnp.exp(-decay_rates[:, None, None] * jnp.maximum(distance, 0.0)[None])
    allowed = causal[None] & (seg_blocks[:, :, None] == seg_blocks[:, None, :])
    decay_mat = jnp.where(allowed[:, None], base_decay[None], 0.0)
    scores = jnp.einsum("bthd,bshd->bhts", q_blocks, k_blocks, preferred_element_type=jnp.float32)
    weighted = (scores * decay_mat).astype(jnp.bfloat16)
    inside = jnp.einsum("bhts,bshd->bthd", weighted, v_blocks, preferred_element_type=jnp.float32)
    last_segs = seg_blocks[:, -1]
    prev_segs = jnp.concatenate([jnp.reshape(seg_start, (1,)), last_segs[:-1]])
    carry_in = jnp.where(
        (seg_blocks == prev_segs[:, None])[:, :, None],
        jnp.exp(-decay_rates[None, :] * (offsets + 1.0)[:, None])[None],
        0.0,
    )
    keep_end = jnp.where(
        (seg_blocks == last_segs[:, None])[:, :, None],
        jnp.exp(-decay_rates[None, :] * (block_rows - 1.0 - offsets)[:, None])[None],
        0.0,
    )
    whole_keep = jnp.where(
        (last_segs == prev_segs)[:, None], jnp.exp(-decay_rates * block_rows)[None, :], 0.0
    )
    weighted_keys = (k_blocks.astype(jnp.float32) * keep_end[:, :, :, None]).astype(jnp.bfloat16)
    local_states = jnp.einsum(
        "bshd,bshe->bhde", weighted_keys, v_blocks, preferred_element_type=jnp.float32
    )

    def advance(running, pieces):
        kv_state, decay_total = running
        keep_now, state_now = pieces
        following = keep_now[:, None, None] * kv_state + state_now
        return ((following, decay_total * keep_now), kv_state)

    initial = (
        jnp.zeros((heads_dev, head_dim, head_dim), jnp.float32),
        jnp.ones((heads_dev,), jnp.float32),
    )
    finished, entering = lax.scan(advance, initial, (whole_keep, local_states))
    carried = jnp.einsum(
        "bthd,bhde->bthe", q_blocks.astype(jnp.float32), entering, precision=highest
    )
    attended = inside + carried * carry_in[:, :, :, None]
    return (attended.reshape(total_rows, heads_dev, head_dim), finished[0], finished[1])


def combine_states(earlier, later):
    return (earlier[0] * later[0], later[0][:, None, None] * earlier[1] + later[1])


def local(queries, keys, values, decay_rates, norm_gain, out_weight, doc_lengths):
    highest = lax.Precision.HIGHEST
    q_heads, k_heads, v_heads = (
        lax.all_to_all(queries, "tp", split_axis=1, concat_axis=0, tiled=True),
        lax.all_to_all(keys, "tp", split_axis=1, concat_axis=0, tiled=True),
        lax.all_to_all(values, "tp", split_axis=1, concat_axis=0, tiled=True),
    )
    heads_dev = decay_rates.shape[0]
    seq_rows = q_heads.shape[0]
    head_dim = q_heads.shape[1] // heads_dev
    group_size = lax.axis_size("tp")
    first_row = lax.axis_index("seq") * seq_rows
    doc_ends = jnp.cumsum(doc_lengths)
    positions = first_row + jnp.arange(seq_rows, dtype=jnp.int32)
    segments = segment_ids(positions, doc_ends)
    seg_before = segment_ids(jnp.reshape(first_row - 1, (1,)), doc_ends)[0]
    shaped = (seq_rows, heads_dev, head_dim)
    attended, kv_state, decay_total = local_pass(
        q_heads.reshape(shaped),
        k_heads.reshape(shaped),
        v_heads.reshape(shaped),
        segments,
        decay_rates,
        seg_before,
    )
    prefix = carried_in(
        (decay_total, kv_state),
        "seq",
        combine_states,
        (jnp.ones_like(decay_total), jnp.zeros_like(kv_state)),
    )
    incoming = prefix[1]
    steps_in = jnp.arange(seq_rows).astype(jnp.float32) + 1.0
    carry_in = jnp.where(
        (segments == seg_before)[None, :], jnp.exp(-decay_rates[:, None] * steps_in[None, :]), 0.0
    )
    wide_queries = q_heads.reshape(shaped).astype(jnp.float32)
    attended = (
        attended
        + jnp.einsum("thd,hde->the", wide_queries, incoming, precision=highest)
        * carry_in.T[:, :, None]
    )
    flat = attended.reshape(seq_rows, heads_dev * head_dim)
    power_sum = lax.psum(jnp.sum(flat * flat, axis=1), "tp")
    inv_rms = lax.rsqrt(power_sum / (heads_dev * head_dim * group_size) + 1e-06)
    normed = (flat * inv_rms[:, None] * norm_gain[None, :]).astype(jnp.bfloat16)
    return lax.psum_scatter(
        jnp.dot(normed, out_weight, preferred_element_type=jnp.float32)
        .astype(jnp.bfloat16)
        .astype(jnp.float32)
        .astype(jnp.bfloat16),
        "tp",
        scatter_dimension=0,
        tiled=True,
    )

MESH = pl.DeviceIdType.MESH
FAR = 1e12
BLOCK = 256
HEAD_CHUNKS = 4
COL_CHUNKS = 12
HALVES = 2


def layer_kernel(
    seq_count, rates, lengths, gain, q_in, k_in, v_in, w_in, out,
    qb, kb, vb, wb, ab, dist, dist_end, dist_in, states, chain_in, chain_out, power,
    pow_send, pow_recv, scale_rows, prod, first_in, second_out, second_in,
    a2a_send, a2a_recv, q_send, q_recv, own_sem, w_sem, chain_send, chain_recv, pow_ss, pow_rs, fs, fr, ss, sr,
):
    seq, me = lax.axis_index("seq"), lax.axis_index("tp")
    x, y = lax.rem(me, 2), me // 2
    peers = (y * 2 + (1 - x), (1 - y) * 2 + x, (1 - y) * 2 + (1 - x))
    rows, width = q_in.shape[0], kb.shape[1]
    group_rows = kb.shape[0]
    half_rows, half_block = rows // HALVES, BLOCK // HALVES
    heads = width // 128
    chunk_heads = heads // HEAD_CHUNKS
    chunk_cols = width // HEAD_CHUNKS
    out_cols = out.shape[1] // COL_CHUNKS
    blocks = group_rows // BLOCK
    tensors = ((k_in, kb), (v_in, vb))

    barrier = pltpu.get_barrier_semaphore()
    for peer in peers:
        pl.semaphore_signal(barrier, inc=1, device_id={"tp": peer}, device_id_type=MESH)

    @pl.when(seq > 0)
    def _():
        pl.semaphore_signal(barrier, inc=1, device_id={"seq": seq - 1}, device_id_type=MESH)

    @pl.when(seq < seq_count - 1)
    def _():
        pl.semaphore_signal(barrier, inc=1, device_id={"seq": seq + 1}, device_id_type=MESH)

    def own_copy(i):
        src, dst = tensors[i]
        cols = pl.ds(pl.multiple_of(me * width, 128), width)
        return pltpu.make_async_copy(
            src.at[:, cols], dst.at[pl.ds(pl.multiple_of(me * rows, 128), rows)], own_sem.at[i]
        )

    def own_q(r):
        return pltpu.make_async_copy(
            q_in.at[pl.ds(r * half_rows, half_rows), pl.ds(pl.multiple_of(me * width, 128), width)],
            qb.at[r, pl.ds(pl.multiple_of(me * half_rows, half_rows), half_rows)],
            own_sem.at[2 + r],
        )

    for i in range(2):
        own_copy(i).start()
    for r in range(HALVES):
        own_q(r).start()

    before, after = (seq + seq_count - 1) // seq_count, (2 * seq_count - 2 - seq) // seq_count
    pl.semaphore_wait(barrier, 3 + before + after)

    def exchange(i, c, d):
        src, dst = tensors[i]
        peer = peers[d]
        return pltpu.make_async_remote_copy(
            src_ref=src.at[:, pl.ds(pl.multiple_of(peer * width + c * chunk_cols, 128), chunk_cols)],
            dst_ref=dst.at[
                pl.ds(pl.multiple_of(me * rows, 128), rows),
                pl.ds(pl.multiple_of(c * chunk_cols, 128), chunk_cols),
            ],
            send_sem=a2a_send.at[i, c, d],
            recv_sem=a2a_recv.at[i, c, d],
            device_id={"tp": peer},
            device_id_type=MESH,
        )

    def send_kv(c, _):
        for i in (0, 1):
            for d in (2, 0, 1):
                exchange(i, c, d).start()
        return 0

    def exchange_q(r, d):
        peer = peers[d]
        return pltpu.make_async_remote_copy(
            src_ref=q_in.at[
                pl.ds(r * half_rows, half_rows), pl.ds(pl.multiple_of(peer * width, 128), width)
            ],
            dst_ref=qb.at[r, pl.ds(pl.multiple_of(me * half_rows, half_rows), half_rows)],
            send_sem=q_send.at[r, d],
            recv_sem=q_recv.at[r, d],
            device_id={"tp": peer},
            device_id_type=MESH,
        )

    lax.fori_loop(0, HEAD_CHUNKS, send_kv, 0)
    for r in range(HALVES):
        for d in (2, 0, 1):
            exchange_q(r, d).start()
    load_w = pltpu.make_async_copy(w_in, wb, w_sem)
    load_w.start()

    first_row = seq * group_rows
    ends, end = [], jnp.int32(0)
    for j in range(lengths.shape[0]):
        end = end + lengths[j]
        ends.append(end)

    def scalar_seg(position):
        seg = jnp.int32(0)
        for e in ends:
            seg = seg + jnp.where(e <= position, 1, 0)
        return seg

    edge_segs = [scalar_seg(first_row - 1 + b * BLOCK) for b in range(blocks + 1)]
    for b in range(blocks):
        base = first_row + b * BLOCK
        pos_k = lax.broadcasted_iota(jnp.int32, (BLOCK, 128), 0)
        pos_r = lax.broadcasted_iota(jnp.int32, (8, BLOCK), 1)

        def segs(pos):
            seg = jnp.zeros_like(pos)
            for e in ends:
                seg = seg + jnp.where(e - base <= pos, 1, 0)
            return seg

        seg_r = segs(pos_r)
        dist_end[b] = jnp.where(
            segs(pos_k) == edge_segs[b + 1], BLOCK - 1.0 - pos_k.astype(jnp.float32), FAR
        )
        for r in range(HALVES):
            at = lax.broadcasted_iota(jnp.int32, (half_block, 128), 0)
            pos_q = at + r * half_rows
            for edge in range(half_rows, half_block, half_rows):
                pos_q = pos_q + jnp.where(at >= edge, rows - half_rows, 0)
            seg_q = segs(pos_q)
            dist_in[r, b] = jnp.where(
                seg_q == edge_segs[b], pos_q.astype(jnp.float32) + 1.0, FAR
            )
            wide_seg = jnp.concatenate([seg_q] * (BLOCK // 128), axis=1)
            wide_pos = jnp.concatenate([pos_q] * (BLOCK // 128), axis=1)
            gap = wide_pos - lax.broadcasted_iota(jnp.int32, (half_block, BLOCK), 1)
            same = wide_seg == jnp.broadcast_to(seg_r[:1], (half_block, BLOCK))
            dist[r, b] = jnp.where(same & (gap >= 0), gap.astype(jnp.float32), FAR)
    keep_dist = [
        jnp.where(edge_segs[b + 1] == edge_segs[b], jnp.float32(BLOCK), jnp.float32(FAR))
        for b in range(blocks)
    ]

    @pl.when(seq == 0)
    def _():
        chain_in[...] = jnp.zeros_like(chain_in)

    def hop(c):
        return pltpu.make_async_remote_copy(
            src_ref=chain_out.at[c],
            dst_ref=chain_in.at[c],
            send_sem=chain_send.at[c],
            recv_sem=chain_recv.at[c],
            device_id={"seq": lax.rem(seq + 1, seq_count)},
            device_id_type=MESH,
        )

    own_copy(0).wait()
    own_copy(1).wait()

    def state_chunk(c, _):
        for i in (0, 1):
            for d in range(3):
                exchange(i, c, d).wait_recv()
        for g in range(chunk_heads):
            h = c * chunk_heads + g
            cols = pl.ds(pl.multiple_of(h * 128, 128), 128)
            rate = rates[h]
            for b in range(blocks):
                span = pl.ds(b * BLOCK, BLOCK)
                weight = jnp.exp(dist_end[b] * -rate)
                wk = (kb[span, cols].astype(jnp.float32) * weight).astype(jnp.bfloat16)
                states[b, h] = lax.dot_general(
                    wk, vb[span, cols], (((0,), (0,)), ((), ())), preferred_element_type=jnp.float32
                )

        @pl.when(seq > 0)
        def _():
            hop(c).wait_recv()

        for g in range(chunk_heads):
            h = c * chunk_heads + g
            rate = rates[h]
            entering = chain_in[c, g].astype(jnp.float32)
            for b in range(blocks):
                keep = jnp.exp(jnp.full((128, 128), keep_dist[b] * -rate, jnp.float32))
                following = keep * entering + states[b, h]
                states[b, h] = entering
                entering = following
            chain_out[c, g] = entering.astype(jnp.bfloat16)

        @pl.when(seq < seq_count - 1)
        def _():
            hop(c).start()

        return 0

    lax.fori_loop(0, HEAD_CHUNKS, state_chunk, 0)

    power[...] = jnp.zeros_like(power)

    def attend(r):
        own_q(r).wait()
        for d in range(3):
            exchange_q(r, d).wait_recv()

        def attend_chunk(c, _):
            for g in range(chunk_heads):
                h = c * chunk_heads + g
                cols = pl.ds(pl.multiple_of(h * 128, 128), 128)
                rate = rates[h]
                for b in range(blocks):
                    span, mine = pl.ds(b * BLOCK, BLOCK), pl.ds(b * half_block, half_block)
                    q, k, v = qb[r, mine, cols], kb[span, cols], vb[span, cols]
                    scores = lax.dot_general(
                        q, k, (((1,), (1,)), ((), ())), preferred_element_type=jnp.float32
                    )
                    weighted = (scores * jnp.exp(dist[r, b] * -rate)).astype(jnp.bfloat16)
                    inside = jnp.dot(weighted, v, preferred_element_type=jnp.float32)
                    carried = jnp.dot(
                        q, states[b, h].astype(jnp.bfloat16), preferred_element_type=jnp.float32
                    )
                    attended = inside + carried * jnp.exp(dist_in[r, b] * -rate)
                    power[r, mine] += attended * attended
                    ab[r, mine, cols] = (attended * gain[cols]).astype(jnp.bfloat16)
            return 0

        lax.fori_loop(0, HEAD_CHUNKS, attend_chunk, 0)

    attend(0)
    load_w.wait()

    def ways(c):
        odd = lax.rem(c, 2)
        p1 = peers[0] * (1 - odd) + peers[1] * odd
        p2 = peers[1] * (1 - odd) + peers[0] * odd
        return p1, p2

    def first_hop(c, which):
        p1, _ = ways(c)
        return pltpu.make_async_remote_copy(
            src_ref=prod.at[c, p1 if which == 0 else peers[2]],
            dst_ref=first_in.at[c, which],
            send_sem=fs.at[c, which],
            recv_sem=fr.at[c, which],
            device_id={"tp": p1},
            device_id_type=MESH,
        )

    def second_hop(c):
        _, p2 = ways(c)
        return pltpu.make_async_remote_copy(
            src_ref=second_out.at[c],
            dst_ref=second_in.at[c],
            send_sem=ss.at[c],
            recv_sem=sr.at[c],
            device_id={"tp": p2},
            device_id_type=MESH,
        )

    def pow_copy(d):
        return pltpu.make_async_remote_copy(
            src_ref=pow_send.at[peers[d]],
            dst_ref=pow_recv.at[d],
            send_sem=pow_ss.at[d],
            recv_sem=pow_rs.at[d],
            device_id={"tp": peers[d]},
            device_id_type=MESH,
        )

    def project(c):
        cols = pl.ds(pl.multiple_of(lax.rem(c, COL_CHUNKS) * out_cols, 128), out_cols)
        part = jnp.dot(ab[c // COL_CHUNKS], wb[:, cols], preferred_element_type=jnp.float32)
        prod[c] = part.astype(jnp.bfloat16).reshape(prod.shape[1:])
        first_hop(c, 1).start()

    def forward(c):
        _, p2 = ways(c)
        first_hop(c, 1).wait_recv()
        second_out[c] = (
            prod[c, p2].astype(jnp.float32) + first_in[c, 1].astype(jnp.float32)
        ).astype(jnp.bfloat16)
        second_hop(c).start()
        first_hop(c, 0).start()

    def finish(c):
        first_hop(c, 0).wait_recv()
        second_hop(c).wait_recv()
        summed = (
            prod[c, me].astype(jnp.float32)
            + first_in[c, 0].astype(jnp.float32)
            + second_in[c].astype(jnp.float32)
        )
        r = c // COL_CHUNKS
        cols = pl.ds(pl.multiple_of(lax.rem(c, COL_CHUNKS) * out_cols, 128), out_cols)
        span = pl.ds(pl.multiple_of(r * half_rows, half_rows), half_rows)
        out[span, cols] = (summed * scale_rows[r]).astype(jnp.bfloat16)

    def lead(c, _):
        project(c)
        return 0

    def steady(c, _):
        project(c)
        forward(c - COL_CHUNKS)
        return 0

    def trail(c, _):
        forward(c)
        finish(c - COL_CHUNKS)
        return 0

    def last(c, _):
        finish(c)
        return 0

    units = HALVES * COL_CHUNKS
    lax.fori_loop(0, COL_CHUNKS, lead, 0)
    attend(1)
    for j in range(4):
        own_rows = [power[r, pl.ds(j * half_rows, half_rows)] for r in range(HALVES)]
        row = jnp.sum(jnp.concatenate(own_rows, axis=0).T, axis=0, keepdims=True)
        pow_send[j] = jnp.broadcast_to(row, pow_send.shape[1:])
    for d in range(3):
        pow_copy(d).start()
    lax.fori_loop(COL_CHUNKS, units, steady, 0)

    total = pow_send[me]
    for d in range(3):
        pow_copy(d).wait_recv()
        total = total + pow_recv[d]
    scale = lax.rsqrt(total / (4 * width) + 1e-06)
    scale = jnp.broadcast_to(scale[:1], (128, rows)).T
    for r in range(HALVES):
        part = scale[r * half_rows : (r + 1) * half_rows]
        scale_rows[r] = jnp.concatenate([part] * (out_cols // 128), axis=1)

    lax.fori_loop(COL_CHUNKS, units, trail, 0)
    lax.fori_loop(COL_CHUNKS, units, last, 0)

    def drain_heads(c, _):
        for i in range(2):
            for d in range(3):
                exchange(i, c, d).wait_send()

        @pl.when(seq < seq_count - 1)
        def _():
            hop(c).wait_send()

        return 0

    def drain_cols(c, _):
        first_hop(c, 0).wait_send()
        first_hop(c, 1).wait_send()
        second_hop(c).wait_send()
        return 0

    lax.fori_loop(0, HEAD_CHUNKS, drain_heads, 0)
    lax.fori_loop(0, units, drain_cols, 0)
    for r in range(HALVES):
        for d in range(3):
            exchange_q(r, d).wait_send()
    for d in range(3):
        pow_copy(d).wait_send()


def fused(queries, keys, values, decay_rates, norm_gain, out_weight, doc_lengths):
    rows, model = queries.shape
    width, out_width = out_weight.shape
    heads = width // 128
    group = rows * 4
    blocks = group // BLOCK
    per = heads // HEAD_CHUNKS
    cols = out_width // COL_CHUNKS
    units, half = HALVES * COL_CHUNKS, rows // HALVES
    bf16, f32 = jnp.bfloat16, jnp.float32
    hbm, vmem = pl.BlockSpec(memory_space=pl.ANY), pl.BlockSpec(memory_space=pltpu.VMEM)
    smem = pl.BlockSpec(memory_space=pltpu.SMEM)
    dma = pltpu.SemaphoreType.DMA
    return pl.pallas_call(
        functools.partial(layer_kernel, lax.axis_size("seq")),
        out_shape=jax.ShapeDtypeStruct((rows, out_width), bf16),
        in_specs=[smem, smem, vmem, hbm, hbm, hbm, hbm],
        out_specs=vmem,
        scratch_shapes=[
            pltpu.VMEM((HALVES, group // HALVES, width), bf16),
            pltpu.VMEM((group, width), bf16),
            pltpu.VMEM((group, width), bf16),
            pltpu.VMEM((width, out_width), bf16),
            pltpu.VMEM((HALVES, group // HALVES, width), bf16),
            pltpu.VMEM((HALVES, blocks, BLOCK // HALVES, BLOCK), f32),
            pltpu.VMEM((blocks, BLOCK, 128), f32),
            pltpu.VMEM((HALVES, blocks, BLOCK // HALVES, 128), f32),
            pltpu.VMEM((blocks, heads, 128, 128), f32),
            pltpu.VMEM((HEAD_CHUNKS, per, 128, 128), bf16),
            pltpu.VMEM((HEAD_CHUNKS, per, 128, 128), bf16),
            pltpu.VMEM((HALVES, group // HALVES, 128), f32),
            pltpu.VMEM((4, 8, rows), f32),
            pltpu.VMEM((3, 8, rows), f32),
            pltpu.VMEM((HALVES, half, cols), f32),
            pltpu.VMEM((units, 4, half, cols), bf16),
            pltpu.VMEM((units, 2, half, cols), bf16),
            pltpu.VMEM((units, half, cols), bf16),
            pltpu.VMEM((units, half, cols), bf16),
            dma((2, HEAD_CHUNKS, 3)),
            dma((2, HEAD_CHUNKS, 3)),
            dma((HALVES, 3)),
            dma((HALVES, 3)),
            dma((2 + HALVES,)),
            dma,
            dma((HEAD_CHUNKS,)),
            dma((HEAD_CHUNKS,)),
            dma((3,)),
            dma((3,)),
            dma((units, 2)),
            dma((units, 2)),
            dma((units,)),
            dma((units,)),
        ],
        compiler_params=pltpu.CompilerParams(
            collective_id=0, has_side_effects=True, vmem_limit_bytes=58 * 2**20
        ),
        name="layer",
    )(decay_rates, doc_lengths, norm_gain, queries, keys, values, out_weight)


def solution(mesh):
    return jax.shard_map(
        fused if mesh.shape["tp"] == 4 else local,
        mesh=mesh,
        in_specs=(
            P(("seq", "tp"), None),
            P(("seq", "tp"), None),
            P(("seq", "tp"), None),
            P("tp"),
            P("tp"),
            P("tp", None),
            P(),
        ),
        out_specs=P(("seq", "tp"), None),
        check_vma=False,
    )
```

```python
import functools

import jax
import jax.numpy as jnp
from jax import lax
from jax.experimental import pallas as pl
from jax.experimental.pallas import tpu as pltpu
from jax.sharding import PartitionSpec as P


def carried_in(x, axis, combine, identity):
    count, position = (lax.axis_size(axis), lax.axis_index(axis))
    everything = jax.tree.map(
        lambda part, kind: lax.all_gather(part.astype(kind), axis), x, (jnp.bfloat16, jnp.bfloat16)
    )
    start = jax.tree.map(
        lambda part, zero: jnp.broadcast_to(jnp.asarray(zero, part.dtype), part.shape), x, identity
    )

    def step(k, before):
        reached = k < position
        new = combine(
            before, jax.tree.map(lambda part, own: part[k].astype(own.dtype), everything, x)
        )
        return jax.tree.map(lambda a, b: jnp.where(reached, a, b), new, before)

    return lax.fori_loop(0, count, step, start)


def segment_ids(positions, doc_ends):
    return jnp.sum((doc_ends[None, :] <= positions[:, None]).astype(jnp.int32), axis=1)


def local_pass(q_heads, k_heads, v_heads, segments, decay_rates, seg_start):
    highest = lax.Precision.HIGHEST
    total_rows, heads_dev, head_dim = q_heads.shape
    block_rows = min(256, total_rows)
    block_count = total_rows // block_rows
    shape_four = (block_count, block_rows, heads_dev, head_dim)
    q_blocks = q_heads.reshape(shape_four)
    k_blocks = k_heads.reshape(shape_four)
    v_blocks = v_heads.reshape(shape_four)
    seg_blocks = segments.reshape(block_count, block_rows)
    offsets = jnp.arange(block_rows).astype(jnp.float32)
    distance = offsets[:, None] - offsets[None, :]
    causal = distance >= 0
    base_decay = jnp.exp(-decay_rates[:, None, None] * jnp.maximum(distance, 0.0)[None])
    allowed = causal[None] & (seg_blocks[:, :, None] == seg_blocks[:, None, :])
    decay_mat = jnp.where(allowed[:, None], base_decay[None], 0.0)
    scores = jnp.einsum("bthd,bshd->bhts", q_blocks, k_blocks, preferred_element_type=jnp.float32)
    weighted = (scores * decay_mat).astype(jnp.bfloat16)
    inside = jnp.einsum("bhts,bshd->bthd", weighted, v_blocks, preferred_element_type=jnp.float32)
    last_segs = seg_blocks[:, -1]
    prev_segs = jnp.concatenate([jnp.reshape(seg_start, (1,)), last_segs[:-1]])
    carry_in = jnp.where(
        (seg_blocks == prev_segs[:, None])[:, :, None],
        jnp.exp(-decay_rates[None, :] * (offsets + 1.0)[:, None])[None],
        0.0,
    )
    keep_end = jnp.where(
        (seg_blocks == last_segs[:, None])[:, :, None],
        jnp.exp(-decay_rates[None, :] * (block_rows - 1.0 - offsets)[:, None])[None],
        0.0,
    )
    whole_keep = jnp.where(
        (last_segs == prev_segs)[:, None], jnp.exp(-decay_rates * block_rows)[None, :], 0.0
    )
    weighted_keys = (k_blocks.astype(jnp.float32) * keep_end[:, :, :, None]).astype(jnp.bfloat16)
    local_states = jnp.einsum(
        "bshd,bshe->bhde", weighted_keys, v_blocks, preferred_element_type=jnp.float32
    )

    def advance(running, pieces):
        kv_state, decay_total = running
        keep_now, state_now = pieces
        following = keep_now[:, None, None] * kv_state + state_now
        return ((following, decay_total * keep_now), kv_state)

    initial = (
        jnp.zeros((heads_dev, head_dim, head_dim), jnp.float32),
        jnp.ones((heads_dev,), jnp.float32),
    )
    finished, entering = lax.scan(advance, initial, (whole_keep, local_states))
    carried = jnp.einsum(
        "bthd,bhde->bthe", q_blocks.astype(jnp.float32), entering, precision=highest
    )
    attended = inside + carried * carry_in[:, :, :, None]
    return (attended.reshape(total_rows, heads_dev, head_dim), finished[0], finished[1])


def combine_states(earlier, later):
    return (earlier[0] * later[0], later[0][:, None, None] * earlier[1] + later[1])


def local(queries, keys, values, decay_rates, norm_gain, out_weight, doc_lengths):
    highest = lax.Precision.HIGHEST
    q_heads, k_heads, v_heads = (
        lax.all_to_all(queries, "tp", split_axis=1, concat_axis=0, tiled=True),
        lax.all_to_all(keys, "tp", split_axis=1, concat_axis=0, tiled=True),
        lax.all_to_all(values, "tp", split_axis=1, concat_axis=0, tiled=True),
    )
    heads_dev = decay_rates.shape[0]
    seq_rows = q_heads.shape[0]
    head_dim = q_heads.shape[1] // heads_dev
    group_size = lax.axis_size("tp")
    first_row = lax.axis_index("seq") * seq_rows
    doc_ends = jnp.cumsum(doc_lengths)
    positions = first_row + jnp.arange(seq_rows, dtype=jnp.int32)
    segments = segment_ids(positions, doc_ends)
    seg_before = segment_ids(jnp.reshape(first_row - 1, (1,)), doc_ends)[0]
    shaped = (seq_rows, heads_dev, head_dim)
    attended, kv_state, decay_total = local_pass(
        q_heads.reshape(shaped),
        k_heads.reshape(shaped),
        v_heads.reshape(shaped),
        segments,
        decay_rates,
        seg_before,
    )
    prefix = carried_in(
        (decay_total, kv_state),
        "seq",
        combine_states,
        (jnp.ones_like(decay_total), jnp.zeros_like(kv_state)),
    )
    incoming = prefix[1]
    steps_in = jnp.arange(seq_rows).astype(jnp.float32) + 1.0
    carry_in = jnp.where(
        (segments == seg_before)[None, :], jnp.exp(-decay_rates[:, None] * steps_in[None, :]), 0.0
    )
    wide_queries = q_heads.reshape(shaped).astype(jnp.float32)
    attended = (
        attended
        + jnp.einsum("thd,hde->the", wide_queries, incoming, precision=highest)
        * carry_in.T[:, :, None]
    )
    flat = attended.reshape(seq_rows, heads_dev * head_dim)
    power_sum = lax.psum(jnp.sum(flat * flat, axis=1), "tp")
    inv_rms = lax.rsqrt(power_sum / (heads_dev * head_dim * group_size) + 1e-06)
    normed = (flat * inv_rms[:, None] * norm_gain[None, :]).astype(jnp.bfloat16)
    return lax.psum_scatter(
        jnp.dot(normed, out_weight, preferred_element_type=jnp.float32)
        .astype(jnp.bfloat16)
        .astype(jnp.float32)
        .astype(jnp.bfloat16),
        "tp",
        scatter_dimension=0,
        tiled=True,
    )

MESH = pl.DeviceIdType.MESH
FAR = 1e12
BLOCK = 256
HEAD_CHUNKS = 4
COL_CHUNKS = 6
HALVES = 2


def layer_kernel(
    seq_count, rates, lengths, gain, q_in, k_in, v_in, w_in, out,
    qb, kb, vb, wb, ab, dist, dist_end, dist_in, states, chain_in, chain_out, power,
    pow_send, pow_recv, scale_rows, prod, first_in, second_out, second_in,
    a2a_send, a2a_recv, q_send, q_recv, own_sem, w_sem, chain_send, chain_recv, pow_ss, pow_rs, fs, fr, ss, sr,
):
    seq, me = lax.axis_index("seq"), lax.axis_index("tp")
    x, y = lax.rem(me, 2), me // 2
    peers = (y * 2 + (1 - x), (1 - y) * 2 + x, (1 - y) * 2 + (1 - x))
    rows, width = q_in.shape[0], kb.shape[1]
    group_rows = kb.shape[0]
    half_rows, half_block = rows // HALVES, BLOCK // HALVES
    heads = width // 128
    chunk_heads = heads // HEAD_CHUNKS
    chunk_cols = width // HEAD_CHUNKS
    out_cols = out.shape[1] // COL_CHUNKS
    blocks = group_rows // BLOCK
    tensors = ((k_in, kb), (v_in, vb))

    barrier = pltpu.get_barrier_semaphore()
    for peer in peers:
        pl.semaphore_signal(barrier, inc=1, device_id={"tp": peer}, device_id_type=MESH)

    @pl.when(seq > 0)
    def _():
        pl.semaphore_signal(barrier, inc=1, device_id={"seq": seq - 1}, device_id_type=MESH)

    @pl.when(seq < seq_count - 1)
    def _():
        pl.semaphore_signal(barrier, inc=1, device_id={"seq": seq + 1}, device_id_type=MESH)

    def own_copy(i):
        src, dst = tensors[i]
        cols = pl.ds(pl.multiple_of(me * width, 128), width)
        return pltpu.make_async_copy(
            src.at[:, cols], dst.at[pl.ds(pl.multiple_of(me * rows, 128), rows)], own_sem.at[i]
        )

    def own_q(r):
        return pltpu.make_async_copy(
            q_in.at[pl.ds(r * half_rows, half_rows), pl.ds(pl.multiple_of(me * width, 128), width)],
            qb.at[r, pl.ds(pl.multiple_of(me * half_rows, half_rows), half_rows)],
            own_sem.at[2 + r],
        )

    for i in range(2):
        own_copy(i).start()
    for r in range(HALVES):
        own_q(r).start()

    before, after = (seq + seq_count - 1) // seq_count, (2 * seq_count - 2 - seq) // seq_count
    pl.semaphore_wait(barrier, 3 + before + after)

    def exchange(i, c, d):
        src, dst = tensors[i]
        peer = peers[d]
        return pltpu.make_async_remote_copy(
            src_ref=src.at[:, pl.ds(pl.multiple_of(peer * width + c * chunk_cols, 128), chunk_cols)],
            dst_ref=dst.at[
                pl.ds(pl.multiple_of(me * rows, 128), rows),
                pl.ds(pl.multiple_of(c * chunk_cols, 128), chunk_cols),
            ],
            send_sem=a2a_send.at[i, c, d],
            recv_sem=a2a_recv.at[i, c, d],
            device_id={"tp": peer},
            device_id_type=MESH,
        )

    def send_kv(c, _):
        for i in (0, 1):
            for d in (2, 0, 1):
                exchange(i, c, d).start()
        return 0

    def exchange_q(r, d):
        peer = peers[d]
        return pltpu.make_async_remote_copy(
            src_ref=q_in.at[
                pl.ds(r * half_rows, half_rows), pl.ds(pl.multiple_of(peer * width, 128), width)
            ],
            dst_ref=qb.at[r, pl.ds(pl.multiple_of(me * half_rows, half_rows), half_rows)],
            send_sem=q_send.at[r, d],
            recv_sem=q_recv.at[r, d],
            device_id={"tp": peer},
            device_id_type=MESH,
        )

    lax.fori_loop(0, HEAD_CHUNKS, send_kv, 0)
    for r in range(HALVES):
        for d in (2, 0, 1):
            exchange_q(r, d).start()
    load_w = pltpu.make_async_copy(w_in, wb, w_sem)
    load_w.start()

    first_row = seq * group_rows
    ends, end = [], jnp.int32(0)
    for j in range(lengths.shape[0]):
        end = end + lengths[j]
        ends.append(end)

    def scalar_seg(position):
        seg = jnp.int32(0)
        for e in ends:
            seg = seg + jnp.where(e <= position, 1, 0)
        return seg

    edge_segs = [scalar_seg(first_row - 1 + b * BLOCK) for b in range(blocks + 1)]
    for b in range(blocks):
        base = first_row + b * BLOCK
        pos_k = lax.broadcasted_iota(jnp.int32, (BLOCK, 128), 0)
        pos_r = lax.broadcasted_iota(jnp.int32, (8, BLOCK), 1)

        def segs(pos):
            seg = jnp.zeros_like(pos)
            for e in ends:
                seg = seg + jnp.where(e - base <= pos, 1, 0)
            return seg

        seg_r = segs(pos_r)
        dist_end[b] = jnp.where(
            segs(pos_k) == edge_segs[b + 1], BLOCK - 1.0 - pos_k.astype(jnp.float32), FAR
        )
        for r in range(HALVES):
            at = lax.broadcasted_iota(jnp.int32, (half_block, 128), 0)
            pos_q = at + r * half_rows
            for edge in range(half_rows, half_block, half_rows):
                pos_q = pos_q + jnp.where(at >= edge, rows - half_rows, 0)
            seg_q = segs(pos_q)
            dist_in[r, b] = jnp.where(
                seg_q == edge_segs[b], pos_q.astype(jnp.float32) + 1.0, FAR
            )
            wide_seg = jnp.concatenate([seg_q] * (BLOCK // 128), axis=1)
            wide_pos = jnp.concatenate([pos_q] * (BLOCK // 128), axis=1)
            gap = wide_pos - lax.broadcasted_iota(jnp.int32, (half_block, BLOCK), 1)
            same = wide_seg == jnp.broadcast_to(seg_r[:1], (half_block, BLOCK))
            dist[r, b] = jnp.where(same & (gap >= 0), gap.astype(jnp.float32), FAR)
    keep_dist = [
        jnp.where(edge_segs[b + 1] == edge_segs[b], jnp.float32(BLOCK), jnp.float32(FAR))
        for b in range(blocks)
    ]

    @pl.when(seq == 0)
    def _():
        chain_in[...] = jnp.zeros_like(chain_in)

    def hop(c):
        return pltpu.make_async_remote_copy(
            src_ref=chain_out.at[c],
            dst_ref=chain_in.at[c],
            send_sem=chain_send.at[c],
            recv_sem=chain_recv.at[c],
            device_id={"seq": lax.rem(seq + 1, seq_count)},
            device_id_type=MESH,
        )

    own_copy(0).wait()
    own_copy(1).wait()

    def state_chunk(c, _):
        for i in (0, 1):
            for d in range(3):
                exchange(i, c, d).wait_recv()
        for g in range(chunk_heads):
            h = c * chunk_heads + g
            cols = pl.ds(pl.multiple_of(h * 128, 128), 128)
            rate = rates[h]
            for b in range(blocks):
                span = pl.ds(b * BLOCK, BLOCK)
                weight = jnp.exp(dist_end[b] * -rate)
                wk = (kb[span, cols].astype(jnp.float32) * weight).astype(jnp.bfloat16)
                states[b, h] = lax.dot_general(
                    wk, vb[span, cols], (((0,), (0,)), ((), ())), preferred_element_type=jnp.float32
                )

        @pl.when(seq > 0)
        def _():
            hop(c).wait_recv()

        for g in range(chunk_heads):
            h = c * chunk_heads + g
            rate = rates[h]
            entering = chain_in[c, g].astype(jnp.float32)
            for b in range(blocks):
                keep = jnp.exp(jnp.full((128, 128), keep_dist[b] * -rate, jnp.float32))
                following = keep * entering + states[b, h]
                states[b, h] = entering
                entering = following
            chain_out[c, g] = entering.astype(jnp.bfloat16)

        @pl.when(seq < seq_count - 1)
        def _():
            hop(c).start()

        return 0

    lax.fori_loop(0, HEAD_CHUNKS, state_chunk, 0)

    power[...] = jnp.zeros_like(power)

    def attend(r):
        own_q(r).wait()
        for d in range(3):
            exchange_q(r, d).wait_recv()

        def attend_chunk(c, _):
            for g in range(chunk_heads):
                h = c * chunk_heads + g
                cols = pl.ds(pl.multiple_of(h * 128, 128), 128)
                rate = rates[h]
                for b in range(blocks):
                    span, mine = pl.ds(b * BLOCK, BLOCK), pl.ds(b * half_block, half_block)
                    q, k, v = qb[r, mine, cols], kb[span, cols], vb[span, cols]
                    scores = lax.dot_general(
                        q, k, (((1,), (1,)), ((), ())), preferred_element_type=jnp.float32
                    )
                    weighted = (scores * jnp.exp(dist[r, b] * -rate)).astype(jnp.bfloat16)
                    inside = jnp.dot(weighted, v, preferred_element_type=jnp.float32)
                    carried = jnp.dot(
                        q, states[b, h].astype(jnp.bfloat16), preferred_element_type=jnp.float32
                    )
                    attended = inside + carried * jnp.exp(dist_in[r, b] * -rate)
                    power[r, mine] += attended * attended
                    ab[r, mine, cols] = (attended * gain[cols]).astype(jnp.bfloat16)
            return 0

        lax.fori_loop(0, HEAD_CHUNKS, attend_chunk, 0)

    attend(0)
    load_w.wait()

    def ways(c):
        odd = lax.rem(c, 2)
        p1 = peers[0] * (1 - odd) + peers[1] * odd
        p2 = peers[1] * (1 - odd) + peers[0] * odd
        return p1, p2

    def first_hop(c, which):
        p1, _ = ways(c)
        return pltpu.make_async_remote_copy(
            src_ref=prod.at[c, p1 if which == 0 else peers[2]],
            dst_ref=first_in.at[c, which],
            send_sem=fs.at[c, which],
            recv_sem=fr.at[c, which],
            device_id={"tp": p1},
            device_id_type=MESH,
        )

    def second_hop(c):
        _, p2 = ways(c)
        return pltpu.make_async_remote_copy(
            src_ref=second_out.at[c],
            dst_ref=second_in.at[c],
            send_sem=ss.at[c],
            recv_sem=sr.at[c],
            device_id={"tp": p2},
            device_id_type=MESH,
        )

    def pow_copy(d):
        return pltpu.make_async_remote_copy(
            src_ref=pow_send.at[peers[d]],
            dst_ref=pow_recv.at[d],
            send_sem=pow_ss.at[d],
            recv_sem=pow_rs.at[d],
            device_id={"tp": peers[d]},
            device_id_type=MESH,
        )

    def project(c):
        cols = pl.ds(pl.multiple_of(lax.rem(c, COL_CHUNKS) * out_cols, 128), out_cols)
        part = jnp.dot(ab[c // COL_CHUNKS], wb[:, cols], preferred_element_type=jnp.float32)
        prod[c] = part.astype(jnp.bfloat16).reshape(prod.shape[1:])
        first_hop(c, 1).start()

    def forward(c):
        _, p2 = ways(c)
        first_hop(c, 1).wait_recv()
        second_out[c] = (
            prod[c, p2].astype(jnp.float32) + first_in[c, 1].astype(jnp.float32)
        ).astype(jnp.bfloat16)
        second_hop(c).start()
        first_hop(c, 0).start()

    def finish(c):
        first_hop(c, 0).wait_recv()
        second_hop(c).wait_recv()
        summed = (
            prod[c, me].astype(jnp.float32)
            + first_in[c, 0].astype(jnp.float32)
            + second_in[c].astype(jnp.float32)
        )
        r = c // COL_CHUNKS
        cols = pl.ds(pl.multiple_of(lax.rem(c, COL_CHUNKS) * out_cols, 128), out_cols)
        span = pl.ds(pl.multiple_of(r * half_rows, half_rows), half_rows)
        out[span, cols] = (summed * scale_rows[r]).astype(jnp.bfloat16)

    def lead(c, _):
        project(c)
        return 0

    def steady(c, _):
        project(c)
        forward(c - COL_CHUNKS)
        return 0

    def trail(c, _):
        forward(c)
        finish(c - COL_CHUNKS)
        return 0

    def last(c, _):
        finish(c)
        return 0

    units = HALVES * COL_CHUNKS
    lax.fori_loop(0, COL_CHUNKS, lead, 0)
    attend(1)
    for j in range(4):
        own_rows = [power[r, pl.ds(j * half_rows, half_rows)] for r in range(HALVES)]
        row = jnp.sum(jnp.concatenate(own_rows, axis=0).T, axis=0, keepdims=True)
        pow_send[j] = jnp.broadcast_to(row, pow_send.shape[1:])
    for d in range(3):
        pow_copy(d).start()
    lax.fori_loop(COL_CHUNKS, units, steady, 0)

    total = pow_send[me]
    for d in range(3):
        pow_copy(d).wait_recv()
        total = total + pow_recv[d]
    scale = lax.rsqrt(total / (4 * width) + 1e-06)
    scale = jnp.broadcast_to(scale[:1], (128, rows)).T
    for r in range(HALVES):
        part = scale[r * half_rows : (r + 1) * half_rows]
        scale_rows[r] = jnp.concatenate([part] * (out_cols // 128), axis=1)

    lax.fori_loop(COL_CHUNKS, units, trail, 0)
    lax.fori_loop(COL_CHUNKS, units, last, 0)

    def drain_heads(c, _):
        for i in range(2):
            for d in range(3):
                exchange(i, c, d).wait_send()

        @pl.when(seq < seq_count - 1)
        def _():
            hop(c).wait_send()

        return 0

    def drain_cols(c, _):
        first_hop(c, 0).wait_send()
        first_hop(c, 1).wait_send()
        second_hop(c).wait_send()
        return 0

    lax.fori_loop(0, HEAD_CHUNKS, drain_heads, 0)
    lax.fori_loop(0, units, drain_cols, 0)
    for r in range(HALVES):
        for d in range(3):
            exchange_q(r, d).wait_send()
    for d in range(3):
        pow_copy(d).wait_send()


def fused(queries, keys, values, decay_rates, norm_gain, out_weight, doc_lengths):
    rows, model = queries.shape
    width, out_width = out_weight.shape
    heads = width // 128
    group = rows * 4
    blocks = group // BLOCK
    per = heads // HEAD_CHUNKS
    cols = out_width // COL_CHUNKS
    units, half = HALVES * COL_CHUNKS, rows // HALVES
    bf16, f32 = jnp.bfloat16, jnp.float32
    hbm, vmem = pl.BlockSpec(memory_space=pl.ANY), pl.BlockSpec(memory_space=pltpu.VMEM)
    smem = pl.BlockSpec(memory_space=pltpu.SMEM)
    dma = pltpu.SemaphoreType.DMA
    return pl.pallas_call(
        functools.partial(layer_kernel, lax.axis_size("seq")),
        out_shape=jax.ShapeDtypeStruct((rows, out_width), bf16),
        in_specs=[smem, smem, vmem, hbm, hbm, hbm, hbm],
        out_specs=vmem,
        scratch_shapes=[
            pltpu.VMEM((HALVES, group // HALVES, width), bf16),
            pltpu.VMEM((group, width), bf16),
            pltpu.VMEM((group, width), bf16),
            pltpu.VMEM((width, out_width), bf16),
            pltpu.VMEM((HALVES, group // HALVES, width), bf16),
            pltpu.VMEM((HALVES, blocks, BLOCK // HALVES, BLOCK), f32),
            pltpu.VMEM((blocks, BLOCK, 128), f32),
            pltpu.VMEM((HALVES, blocks, BLOCK // HALVES, 128), f32),
            pltpu.VMEM((blocks, heads, 128, 128), f32),
            pltpu.VMEM((HEAD_CHUNKS, per, 128, 128), bf16),
            pltpu.VMEM((HEAD_CHUNKS, per, 128, 128), bf16),
            pltpu.VMEM((HALVES, group // HALVES, 128), f32),
            pltpu.VMEM((4, 8, rows), f32),
            pltpu.VMEM((3, 8, rows), f32),
            pltpu.VMEM((HALVES, half, cols), f32),
            pltpu.VMEM((units, 4, half, cols), bf16),
            pltpu.VMEM((units, 2, half, cols), bf16),
            pltpu.VMEM((units, half, cols), bf16),
            pltpu.VMEM((units, half, cols), bf16),
            dma((2, HEAD_CHUNKS, 3)),
            dma((2, HEAD_CHUNKS, 3)),
            dma((HALVES, 3)),
            dma((HALVES, 3)),
            dma((2 + HALVES,)),
            dma,
            dma((HEAD_CHUNKS,)),
            dma((HEAD_CHUNKS,)),
            dma((3,)),
            dma((3,)),
            dma((units, 2)),
            dma((units, 2)),
            dma((units,)),
            dma((units,)),
        ],
        compiler_params=pltpu.CompilerParams(
            collective_id=0, has_side_effects=True, vmem_limit_bytes=58 * 2**20
        ),
        name="layer",
    )(decay_rates, doc_lengths, norm_gain, queries, keys, values, out_weight)


def solution(mesh):
    return jax.shard_map(
        fused if mesh.shape["tp"] == 4 else local,
        mesh=mesh,
        in_specs=(
            P(("seq", "tp"), None),
            P(("seq", "tp"), None),
            P(("seq", "tp"), None),
            P("tp"),
            P("tp"),
            P("tp", None),
            P(),
        ),
        out_specs=P(("seq", "tp"), None),
        check_vma=False,
    )
```
